128 devices in a mesh: shot: 16 (over z, x), rcv: 8 (over y, core).
Axes of the slice: x: 4, y: 4, z: 4, core: 2. Of those that a mesh axis runs over, the one named last changes fastest.
Arguments:
- traces: bfloat16 [512, 512, 1024], P('shot', 'rcv'), may hold values from -6 to 6
- aperture_lists: int32 [16, 8, 8], P('shot', 'rcv'), may hold values from 0 to 15, as said below
- aperture_counts: int32 [16, 8], P('shot', 'rcv'), may hold values from 4 to 8
Outputs:
- multiples: float32 [64, 2, 512, 512], P(None, None, 'shot', 'rcv')
The draws below stay inside these ranges and needn't reach their ends.
Inputs may be any that keep to these rules, and one draw needn't show every extreme that they name: `aperture_lists`: for tile (i, j), entries 0 to aperture_counts[i, j] - 1 are consecutive rising x-block numbers (block b covers positions b * 32 to (b + 1) * 32 - 1) near the midpoint of the tile's shots and receivers; the other entries are 0.
All inputs are finite; a program needn't handle non-finite values.
Results may differ from the reference program's by a relative error of at most 0.0052.
Values may be sent and summed in bfloat16 or wider, within the bound.
A program may use at most 128 MiB of HBM per device.

```python
import math
import jax
import jax.numpy as jnp
from jax import lax

SHOTS_PER_INDEX = 32
NT = 1024
BAND = 32
APB = 8
FIRST = 32
SECOND = 128
FREQS = 64
N = 512
RC_DEV = 64
XBLOCKS = 16
RECEIVER_TILES = 8


def aperture_tables(key):
    first_key, second_key = jax.random.split(jax.random.fold_in(key, 7))
    shot_index = jnp.arange(XBLOCKS, dtype=jnp.int32)[:, None]
    receiver_index = jnp.arange(RECEIVER_TILES, dtype=jnp.int32)[None, :]
    counts = jax.random.randint(first_key, (XBLOCKS, RECEIVER_TILES), APB // 2, APB + 1).astype(jnp.int32)
    counts = counts.at[XBLOCKS // 2, RECEIVER_TILES // 2].set(APB)
    counts = counts.at[0, 0].set(APB // 2)
    jitter = jax.random.randint(second_key, (XBLOCKS, RECEIVER_TILES), -1, 2).astype(jnp.int32)
    centre = (2 * shot_index * SHOTS_PER_INDEX + 2 * receiver_index * RC_DEV + SHOTS_PER_INDEX + RC_DEV) // (4 * SHOTS_PER_INDEX) + jitter
    first_block = jnp.clip(centre - counts // 2, 0, XBLOCKS - counts)
    first_block = first_block.at[0, 0].set(0)
    first_block = first_block.at[XBLOCKS - 1, RECEIVER_TILES - 1].set(XBLOCKS - counts[XBLOCKS - 1, RECEIVER_TILES - 1])
    position = jnp.arange(APB, dtype=jnp.int32)
    block_list = jnp.where(position[None, None, :] < counts[:, :, None], first_block[:, :, None] + position[None, None, :], 0)
    return (block_list.astype(jnp.int32), counts.astype(jnp.int32))


def draw_aperture_lists(key, part):
    return aperture_tables(key)[0]


def draw_aperture_counts(key, part):
    return aperture_tables(key)[1]


def block_levels(rng, dims, cuts, least, largest):
    level, own = 1.0, jax.random.fold_in(rng, 6)
    for dim, parts in cuts:
        heights = jnp.exp(jax.random.uniform(jax.random.fold_in(own, dim), (parts,), jnp.float32, least / len(cuts), largest / len(cuts)))
        level = level * jnp.repeat(heights, dims[dim] // parts).reshape([-1 if axis == dim else 1 for axis in range(len(dims))])
    return level


def gaussian(stream_key, shape, width, reach, cuts=(), kind=jnp.bfloat16):
    factor_of = block_levels(stream_key, shape, cuts, -0.22, 0.18) if cuts else 1.0
    drawn = jax.random.normal(stream_key, shape, jnp.float32) * width * factor_of
    return jnp.minimum(jnp.maximum(drawn, -reach), reach).astype(kind)


def setup_inputs(seed: int = 0) -> dict:
    arg_keys = jax.random.split(jax.random.key(seed), 4)
    traces = gaussian(arg_keys[0], (N, N, NT), 1.0, 6.0, ((0, 16), (1, 8)))
    aperture_lists = draw_aperture_lists(jax.random.fold_in(arg_keys[3], 71), 0)
    aperture_counts = draw_aperture_counts(jax.random.fold_in(arg_keys[3], 71), 0)
    return dict(traces=traces, aperture_lists=aperture_lists, aperture_counts=aperture_counts)


def dft_table():
    sample = jnp.arange(NT, dtype=jnp.int32)
    freq_bins = jnp.concatenate([FIRST + jnp.arange(BAND, dtype=jnp.int32), SECOND + jnp.arange(BAND, dtype=jnp.int32)])
    phase = (sample[:, None] * freq_bins[None, :] % NT).astype(jnp.float32) * (2.0 * math.pi / NT)
    factor = 1.0 / math.sqrt(NT)
    return (jnp.concatenate([jnp.cos(phase), -jnp.sin(phase)], axis=1) * factor).astype(jnp.bfloat16)

def spectra(traces):
    shots, receivers, samples = traces.shape
    flat = jnp.dot(traces.reshape(shots * receivers, samples), dft_table(), preferred_element_type=jnp.float32)
    flat = flat.astype(jnp.bfloat16)
    return flat.reshape(shots, receivers, 2, FREQS).transpose(3, 2, 0, 1)

def complex_product(left, right):

    def mult(leading_operand, trailing_operand):
        return jnp.einsum('ylp,ypi->yli', leading_operand, trailing_operand, precision=lax.Precision.HIGHEST)
    real_out = mult(left[:, 0], right[:, 0]) - mult(left[:, 1], right[:, 1])
    imag_out = mult(left[:, 0], right[:, 1]) + mult(left[:, 1], right[:, 0])
    return jnp.stack([real_out, imag_out], axis=1)

def reference(traces, aperture_lists, aperture_counts):
    trace_spectrum = spectra(traces).astype(jnp.float32)
    slots = jnp.arange(APB, dtype=jnp.int32)
    live = slots[None, None, :] < aperture_counts[:, :, None]

    def step(carry, block):
        aperture_member = jnp.any(live & (aperture_lists == block), axis=2).astype(jnp.float32)
        spread = jnp.repeat(jnp.repeat(aperture_member, SHOTS_PER_INDEX, axis=0), RC_DEV, axis=1)
        left = lax.dynamic_slice_in_dim(trace_spectrum, block * SHOTS_PER_INDEX, SHOTS_PER_INDEX, 3)
        right = lax.dynamic_slice_in_dim(trace_spectrum, block * SHOTS_PER_INDEX, SHOTS_PER_INDEX, 2)
        return (carry + complex_product(left, right) * spread[None, None], None)
    initial = jnp.zeros((FREQS, 2, N, N), jnp.float32)
    total, unused = lax.scan(step, initial, jnp.arange(XBLOCKS, dtype=jnp.int32))
    return total * (1.0 / math.sqrt(APB * SHOTS_PER_INDEX))
```

```python
import math

import jax
import jax.numpy as jnp
import ml_dtypes
import numpy as np
from jax import lax
from jax.experimental import pallas as pl
from jax.experimental.pallas import tpu as pltpu
from jax.sharding import PartitionSpec as P

MESH = pl.DeviceIdType.MESH

NT = 1024
BAND = 32
APB = 8
FIRST = 32
SECOND = 128
FREQS = 64
TS = 32
TR = 64
NS = 16
NY = 4
CHIPS = 64
SCALE = 1.0 / math.sqrt(APB * TS)
CHUNKS = 4


def dft_table():
    sample = np.arange(NT)
    bins = np.concatenate([FIRST + np.arange(BAND), SECOND + np.arange(BAND)])
    phase = (bins[:, None] * sample[None, :] % NT).astype(np.float32) * np.float32(2.0 * math.pi / NT)
    phase = phase.astype(np.float64)
    factor = 1.0 / math.sqrt(NT)
    return (np.concatenate([np.cos(phase), -np.sin(phase)], axis=0) * factor).astype(np.float32).astype(
        ml_dtypes.bfloat16
    )


def chip_of(shot, y, k):
    z = lax.rem(shot // 4 + k // 16, 4)
    x = lax.rem(lax.rem(shot, 4) + lax.rem(k // 4, 4), 4)
    return z * 4 + x, lax.rem(y + lax.rem(k, 4), 4)


def kernel(
    traces,
    table_hbm,
    lists,
    counts,
    out,
    tr,
    table,
    specf,
    spec,
    grid,
    mtab,
    mexp,
    masked,
    rhat,
    prod,
    back,
    load_sem,
    table_sem,
    send1,
    recv1,
    xsend,
    xrecv,
    send2,
    recv2,
    msend,
    mrecv,
):
    shot = lax.axis_index("shot")
    rcv = lax.axis_index("rcv")
    y = rcv // 2
    core = lax.rem(rcv, 2)
    z, x = shot // 4, lax.rem(shot, 4)
    me = y * NS + shot

    per = TS // CHUNKS
    pltpu.make_async_copy(table_hbm, table, table_sem).start()
    for n in range(CHUNKS):
        pltpu.make_async_copy(
            traces.at[pl.ds(n * per, per)], tr.at[pl.ds(n * per, per)], load_sem.at[n]
        ).start()

    barrier = pltpu.get_barrier_semaphore()
    pl.semaphore_signal(barrier, inc=1, device_id=(shot, y * 2 + 1 - core), device_id_type=MESH)

    def greet(k, carry):
        ts, ty = chip_of(shot, y, k)
        pl.semaphore_signal(barrier, inc=1, device_id=(ts, ty * 2 + core), device_id_type=MESH)
        return carry

    lax.fori_loop(1, CHIPS, greet, 0)

    lane = lax.broadcasted_iota(jnp.int32, (1, 128), 1)
    live = counts[0, 0]
    member = jnp.zeros((1, 128), jnp.float32)
    for k in range(APB):
        block = jnp.where(k < live, lists[0, k], -1)
        member = jnp.where(lane == block, 1.0, member)
    mtab[me] = member

    pl.semaphore_wait(barrier, CHIPS)

    def mask_copy(stage, d):
        if stage == 0:
            rows, to = pl.ds(me, 1), (z * 4 + lax.rem(x + d, 4), rcv)
        elif stage == 1:
            rows, to = pl.ds(y * NS + z * 4, 4), (lax.rem(z + d, 4) * 4 + x, rcv)
        else:
            rows, to = pl.ds(y * NS, NS), (shot, lax.rem(y + d, 4) * 2 + core)
        return pltpu.make_async_remote_copy(
            src_ref=mtab.at[rows],
            dst_ref=mtab.at[rows],
            send_sem=msend.at[stage * 3 + d - 1],
            recv_sem=mrecv.at[stage * 3 + d - 1],
            device_id=to,
            device_id_type=MESH,
        )

    def mask_start(stage):
        for d in (1, 2, 3):
            mask_copy(stage, d).start()

    def mask_wait(stage):
        for d in (1, 2, 3):
            mask_copy(stage, d).wait()

    mask_start(0)

    low = lax.broadcasted_iota(jnp.int32, (FREQS, 128), 1) < TR
    pltpu.make_async_copy(table_hbm, table, table_sem).wait()
    for n in range(CHUNKS):
        pltpu.make_async_copy(
            traces.at[pl.ds(n * per, per)], tr.at[pl.ds(n * per, per)], load_sem.at[n]
        ).wait()

        def transform(g, carry):
            first = n * per + g * 4
            rows = tr[pl.ds(first, 4)].reshape(4 * TR, NT)
            acc = lax.dot_general(
                table[...], rows, (((1,), (1,)), ((), ())), preferred_element_type=jnp.float32
            )
            for p in range(2):
                re = acc[:FREQS, p * 128 : p * 128 + 128]
                im = acc[FREQS:, p * 128 : p * 128 + 128]
                a = jnp.where(low, re, pltpu.roll(im, TR, 1))
                b = jnp.where(low, pltpu.roll(re, TR, 1), im)
                specf[pl.ds(first + 2 * p, FREQS, stride=TS), :] = a
                specf[pl.ds(first + 2 * p + 1, FREQS, stride=TS), :] = b
            return carry

        lax.fori_loop(0, per // 4, transform, 0)

    mask_wait(0)
    mask_start(1)

    def narrow(f, carry):
        spec[f] = specf[pl.ds(pl.multiple_of(f * TS, TS), TS), :].astype(jnp.bfloat16)
        return carry

    lax.fori_loop(0, FREQS, narrow, 0, unroll=8)

    mine = pl.ds(pl.multiple_of(shot * TS, TS), TS)

    def scatter(k, carry):
        ts, ty = chip_of(shot, y, k)
        pltpu.make_async_remote_copy(
            src_ref=spec.at[ty * NS + ts],
            dst_ref=grid.at[core, y, mine],
            send_sem=send1,
            recv_sem=recv1.at[y],
            device_id=(ts, ty * 2 + core),
            device_id_type=MESH,
        ).start()
        return carry

    pltpu.make_async_copy(spec.at[me], grid.at[core, y, mine], recv1.at[y]).start()
    lax.fori_loop(1, CHIPS, scatter, 0)

    mask_wait(1)
    mask_start(2)

    def slab_copy(ty):
        return pltpu.make_async_remote_copy(
            src_ref=grid.at[core, ty],
            dst_ref=grid.at[core, ty],
            send_sem=xsend.at[ty],
            recv_sem=xrecv.at[ty],
            device_id=(shot, y * 2 + 1 - core),
            device_id_type=MESH,
        )

    def forward(d, carry):
        ty = lax.rem(y + 4 - d, 4)
        pltpu.make_async_copy(grid.at[core, ty], grid.at[core, ty], recv1.at[ty]).wait()
        slab_copy(ty).start()
        return carry

    lax.fori_loop(0, NY, forward, 0)

    mask_wait(2)
    block = lax.broadcasted_iota(jnp.int32, (128, 8 * 128), 0)
    column = lax.broadcasted_iota(jnp.int32, (128, 8 * 128), 1)
    expand = jnp.where(block == 2 * (column // 128) + column % TR // TS, 1.0, 0.0).astype(jnp.bfloat16)
    mexp[...] = jnp.dot(
        mtab[...].reshape(CHIPS, 128).astype(jnp.bfloat16), expand, preferred_element_type=jnp.float32
    )

    for ty in range(NY):
        other = grid.at[1 - core, ty]
        pltpu.make_async_copy(other, other, xrecv.at[ty]).wait()

    left64 = lax.broadcasted_iota(jnp.int32, (TR, 128), 1) < TR

    def column_tile(d, carry):
        ty = lax.rem(y + d, 4)
        for j in range(8):
            part = grid[core, ty, j * TR : (j + 1) * TR, :]
            turned = pltpu.roll(part.astype(jnp.float32), TR, 1)
            rhat[j * 128 : j * 128 + TR, :] = part
            rhat[j * 128 + TR : (j + 1) * 128, :] = jnp.where(left64, -turned, turned).astype(jnp.bfloat16)

        def weigh(i, carry):
            rows = pl.ds(pl.multiple_of(i * TS, TS), TS)
            weights = mexp[pl.ds(ty * NS + i, 1), :]
            for j in range(8):
                w = jnp.broadcast_to(weights[:, j * 128 : (j + 1) * 128], (TS, 128)).astype(jnp.bfloat16)
                masked[rows, j * 128 : (j + 1) * 128] = grid[j % 2, j // 2, rows, :] * w
            return carry

        lax.fori_loop(0, NS, weigh, 0)
        prod[ty] = jnp.dot(masked[...], rhat[...], preferred_element_type=jnp.float32).astype(jnp.bfloat16)

        def give(n, carry):
            ts, ty2 = chip_of(shot, y, n * 4 + d)
            pltpu.make_async_remote_copy(
                src_ref=prod.at[ty, pl.ds(pl.multiple_of(ts * TS, TS), TS)],
                dst_ref=back.at[y, shot],
                send_sem=send2,
                recv_sem=recv2.at[d],
                device_id=(ts, ty * 2 + core),
                device_id_type=MESH,
            ).start()
            return carry

        lax.fori_loop(jnp.where(d == 0, 1, 0), NS, give, 0)
        return carry

    lax.fori_loop(0, NY, column_tile, 0)
    pltpu.make_async_copy(prod.at[y, mine], back.at[y, shot], recv2.at[0]).start()

    def collect(d, carry):
        ty = lax.rem(y + 4 - d, 4)
        pltpu.make_async_copy(back.at[ty], back.at[ty], recv2.at[d]).wait()

        def widen(n, carry):
            tile = back[ty, n].astype(jnp.float32)
            out[ty * NS + n, 0] = tile[:, :TR]
            out[ty * NS + n, 1] = pltpu.roll(tile, TR, 1)[:, :TR]
            return carry

        lax.fori_loop(0, NS, widen, 0, unroll=4)
        return carry

    lax.fori_loop(0, NY, collect, 0)

    def slab_sent(ty, carry):
        slab_copy(ty).wait_send()
        return carry

    lax.fori_loop(0, NY, slab_sent, 0)
    sent = spec.at[pl.ds(0, CHIPS - 1)]
    pltpu.make_async_copy(sent, sent, send1).wait()
    pltpu.make_async_copy(sent, sent, send2).wait()


def local(traces, aperture_lists, aperture_counts):
    bf16, f32 = jnp.bfloat16, jnp.float32
    out = pl.pallas_call(
        kernel,
        out_shape=jax.ShapeDtypeStruct((FREQS, 2, TS, TR), f32),
        in_specs=[
            pl.BlockSpec(memory_space=pl.ANY),
            pl.BlockSpec(memory_space=pl.ANY),
            pl.BlockSpec(memory_space=pltpu.SMEM),
            pl.BlockSpec(memory_space=pltpu.SMEM),
        ],
        out_specs=pl.BlockSpec(memory_space=pltpu.VMEM),
        scratch_shapes=[
            pltpu.VMEM((TS, TR, NT), bf16),
            pltpu.VMEM((128, NT), bf16),
            pltpu.VMEM((FREQS * TS, 128), f32),
            pltpu.VMEM((FREQS, TS, 128), bf16),
            pltpu.VMEM((2, NY, NS * TS, 128), bf16),
            pltpu.VMEM((CHIPS, 1, 128), f32),
            pltpu.VMEM((CHIPS, 8 * 128), f32),
            pltpu.VMEM((NS * TS, 8 * 128), bf16),
            pltpu.VMEM((8 * 128, 128), bf16),
            pltpu.VMEM((NY, NS * TS, 128), bf16),
            pltpu.VMEM((NY, NS, TS, 128), bf16),
            pltpu.SemaphoreType.DMA((CHUNKS,)),
            pltpu.SemaphoreType.DMA,
            pltpu.SemaphoreType.DMA,
            pltpu.SemaphoreType.DMA((NY,)),
            pltpu.SemaphoreType.DMA((NY,)),
            pltpu.SemaphoreType.DMA((NY,)),
            pltpu.SemaphoreType.DMA,
            pltpu.SemaphoreType.DMA((NY,)),
            pltpu.SemaphoreType.DMA((9,)),
            pltpu.SemaphoreType.DMA((9,)),
        ],
        compiler_params=pltpu.CompilerParams(
            collective_id=0, has_side_effects=True, vmem_limit_bytes=32 * 2**20
        ),
        cost_estimate=pl.CostEstimate(flops=2**30, bytes_accessed=8 * 2**20, transcendentals=0),
        name="multiples",
    )(traces, jnp.asarray(dft_table()), aperture_lists.reshape(1, APB), aperture_counts)
    return out * SCALE


def solution(mesh):
    placed = (P("shot", "rcv", None), P("shot", "rcv", None), P("shot", "rcv"))
    return jax.shard_map(
        local, mesh=mesh, in_specs=placed, out_specs=P(None, None, "shot", "rcv"), check_vma=False
    )
```

```python
import math

import jax
import jax.numpy as jnp
import ml_dtypes
import numpy as np
from jax import lax
from jax.experimental import pallas as pl
from jax.experimental.pallas import tpu as pltpu
from jax.sharding import PartitionSpec as P

MESH = pl.DeviceIdType.MESH

NT = 1024
BAND = 32
APB = 8
FIRST = 32
SECOND = 128
FREQS = 64
TS = 32
TR = 64
NS = 16
NY = 4
CHIPS = 64
SCALE = 1.0 / math.sqrt(APB * TS)
CHUNKS = 2
PITCH = 40
VMEM_MIB = 50
ORDER = sorted(
    [(a, b, c) for a in range(4) for b in range(4) for c in range(4) if a or b or c],
    key=lambda k: sum(min(d, 4 - d) for d in k),
)
BACK = (2, 1, 3, 0)


def dft_table():
    sample = np.arange(NT)
    bins = np.concatenate([FIRST + np.arange(BAND), SECOND + np.arange(BAND)])
    phase = (bins[:, None] * sample[None, :] % NT).astype(np.float32) * np.float32(2.0 * math.pi / NT)
    phase = phase.astype(np.float64)
    factor = 1.0 / math.sqrt(NT)
    return (np.concatenate([np.cos(phase), -np.sin(phase)], axis=0) * factor).astype(np.float32).astype(
        ml_dtypes.bfloat16
    )


def kernel(
    traces,
    table_hbm,
    lists_hbm,
    counts_hbm,
    out,
    tr,
    table,
    lists,
    counts,
    specf,
    spec,
    grid,
    mtab,
    mrow,
    mask,
    masked,
    rhat,
    acc,
    prod,
    back,
    load_sem,
    table_sem,
    small_sem,
    send1,
    recv1,
    xsend,
    xrecv,
    send2,
    recv2,
    msend,
    mrecv,
):
    shot = lax.axis_index("shot")
    rcv = lax.axis_index("rcv")
    y = rcv // 2
    core = rcv % 2
    z, x = shot // 4, shot % 4
    me = y * NS + shot
    sibling = (shot, y * 2 + 1 - core)
    zs = [(z + d) % 4 * 4 for d in range(4)]
    xs = [(x + d) % 4 for d in range(4)]
    ys = [(y + d) % 4 for d in range(4)]

    per = TS // CHUNKS
    loads = [
        pltpu.make_async_copy(traces.at[pl.ds(n * per, per)], tr.at[pl.ds(n * per, per)], load_sem.at[n])
        for n in range(CHUNKS)
    ]
    table_load = pltpu.make_async_copy(table_hbm, table, table_sem)
    lists_load = pltpu.make_async_copy(lists_hbm, lists, small_sem.at[0])
    counts_load = pltpu.make_async_copy(counts_hbm, counts, small_sem.at[1])
    table_load.start()
    for load in loads:
        load.start()
    lists_load.start()
    counts_load.start()

    barrier = pltpu.get_barrier_semaphore()
    pl.semaphore_signal(barrier, inc=1, device_id=sibling, device_id_type=MESH)
    for dz, dx, dy in ORDER:
        pl.semaphore_signal(
            barrier, inc=1, device_id=(zs[dz] + xs[dx], ys[dy] * 2 + core), device_id_type=MESH
        )

    lists_load.wait()
    counts_load.wait()
    lane = lax.broadcasted_iota(jnp.int32, (1, 128), 1)
    live = counts[0, 0]
    member = jnp.zeros((1, 128), jnp.float32)
    for k in range(APB):
        block = jnp.where(k < live, lists[0, 0, k], -1)
        member = jnp.where(lane == block, 1.0, member)
    mtab[me] = member

    low = lax.broadcasted_iota(jnp.int32, (FREQS, 128), 1) < TR
    table_load.wait()
    for n in range(CHUNKS):
        loads[n].wait()
        rows = tr[n * per : (n + 1) * per].reshape(per * TR, NT)
        flat = lax.dot_general(
            table[...], rows, (((1,), (1,)), ((), ())), preferred_element_type=jnp.float32
        )
        for p in range(per // 2):
            first = n * per + 2 * p
            re = flat[:FREQS, p * 128 : p * 128 + 128]
            im = flat[FREQS:, p * 128 : p * 128 + 128]
            specf[pl.ds(first, FREQS, stride=PITCH), :] = jnp.where(low, re, pltpu.roll(im, TR, 1))
            specf[pl.ds(first + 1, FREQS, stride=PITCH), :] = jnp.where(low, pltpu.roll(re, TR, 1), im)
    spec[...] = specf[...].reshape(FREQS, PITCH, 128)[:, :TS].astype(jnp.bfloat16)

    def mask_copy(stage, d):
        if stage == 0:
            rows, to = pl.ds(me, 1), (zs[0] + xs[d], rcv)
        elif stage == 1:
            rows, to = pl.ds(y * NS + z * 4, 4), (zs[d] + x, rcv)
        else:
            rows, to = pl.ds(y * NS, NS), (shot, ys[d] * 2 + core)
        return pltpu.make_async_remote_copy(
            src_ref=mtab.at[rows],
            dst_ref=mtab.at[rows],
            send_sem=msend.at[stage * 3 + d - 1],
            recv_sem=mrecv.at[stage * 3 + d - 1],
            device_id=to,
            device_id_type=MESH,
        )

    def mask_start(stage):
        for d in (1, 2, 3):
            mask_copy(stage, d).start()

    def mask_wait(stage):
        for d in (1, 2, 3):
            mask_copy(stage, d).wait()

    mine = pl.ds(pl.multiple_of(shot * TS, TS), TS)

    def scatter(dz, dx, dy):
        ts = zs[dz] + xs[dx]
        pltpu.make_async_remote_copy(
            src_ref=spec.at[ys[dy] * NS + ts],
            dst_ref=grid.at[core, y, mine],
            send_sem=send1,
            recv_sem=recv1.at[y],
            device_id=(ts, ys[dy] * 2 + core),
            device_id_type=MESH,
        ).start()

    pl.semaphore_wait(barrier, CHIPS)
    mask_start(0)
    for step in ORDER[:32]:
        scatter(*step)
    mask_wait(0)
    mask_start(1)
    for step in ORDER[32:]:
        scatter(*step)
    pltpu.make_async_copy(spec.at[me], grid.at[core, y, mine], recv1.at[y]).start()
    mask_wait(1)
    mask_start(2)

    block = lax.broadcasted_iota(jnp.int32, (128, 1024), 0)
    column = lax.broadcasted_iota(jnp.int32, (128, 1024), 1)
    tile = column % 512 // 128 * 2 + (column // 512 + core) % 2
    expand = jnp.where(block == 2 * tile + column % TR // TS, 1.0, 0.0).astype(jnp.bfloat16)
    mask_wait(2)
    mrow[...] = jnp.dot(
        mtab[...].reshape(CHIPS, 128).astype(jnp.bfloat16), expand, preferred_element_type=jnp.float32
    )

    def spread(t, carry):
        mask[t] = jnp.broadcast_to(mrow[pl.ds(t, 1), :], (16, 1024)).astype(jnp.bfloat16)
        return carry

    lax.fori_loop(0, CHIPS, spread, 0, unroll=4)

    def slab_copy(ty):
        return pltpu.make_async_remote_copy(
            src_ref=grid.at[core, ty],
            dst_ref=grid.at[core, ty],
            send_sem=xsend.at[ty],
            recv_sem=xrecv.at[ty],
            device_id=sibling,
            device_id_type=MESH,
        )

    for d in (0, 3, 2, 1):
        slab = grid.at[core, ys[d]]
        pltpu.make_async_copy(slab, slab, recv1.at[ys[d]]).wait()
        slab_copy(ys[d]).start()

    left64 = lax.broadcasted_iota(jnp.int32, (TR, 128), 1) < TR

    def half(d, h):
        par = core if h == 0 else 1 - core
        for k in range(NY):
            cols = slice(k * 128, k * 128 + 128)
            left = grid[par, k].reshape(NS, 2, 16, 128)
            weights = mask[pl.ds(ys[d] * NS, NS), :, h * 512 + k * 128 : h * 512 + k * 128 + 128]
            masked[:, cols] = (left * weights[:, None]).reshape(NS * TS, 128)
            first = pl.multiple_of((2 * k + par) * TR, TR)
            part = grid[core, ys[d], pl.ds(first, TR), :]
            turned = pltpu.roll(part.astype(jnp.float32), TR, 1)
            rhat[k * 128 : k * 128 + TR, :] = part
            rhat[k * 128 + TR : (k + 1) * 128, :] = jnp.where(left64, -turned, turned).astype(jnp.bfloat16)
        return jnp.dot(masked[...], rhat[...], preferred_element_type=jnp.float32)

    for d in range(NY):
        acc[d] = half(d, 0)
    for k in range(NY):
        other = grid.at[1 - core, k]
        pltpu.make_async_copy(other, other, xrecv.at[k]).wait()
    for d in BACK:
        ty = ys[d]
        prod[ty] = (acc[d] + half(d, 1)).astype(jnp.bfloat16)
        for dz in range(4):
            for dx in range(4):
                if d or dz or dx:
                    ts = zs[dz] + xs[dx]
                    pltpu.make_async_remote_copy(
                        src_ref=prod.at[ty, pl.ds(pl.multiple_of(ts * TS, TS), TS)],
                        dst_ref=back.at[y, shot],
                        send_sem=send2,
                        recv_sem=recv2.at[d],
                        device_id=(ts, ty * 2 + core),
                        device_id_type=MESH,
                    ).start()
                else:
                    pltpu.make_async_copy(prod.at[y, mine], back.at[y, shot], recv2.at[0]).start()

    for d in BACK:
        ty = ys[-d % 4]
        pltpu.make_async_copy(back.at[ty], back.at[ty], recv2.at[d]).wait()

        def widen(n, carry):
            tile = back[ty, n].astype(jnp.float32)
            out[ty * NS + n, 0] = tile[:, :TR]
            out[ty * NS + n, 1] = pltpu.roll(tile, TR, 1)[:, :TR]
            return carry

        lax.fori_loop(0, NS, widen, 0, unroll=True)

    for k in range(NY):
        slab_copy(k).wait_send()
    sent = spec.at[pl.ds(0, CHIPS - 1)]
    pltpu.make_async_copy(sent, sent, send1).wait()
    pltpu.make_async_copy(sent, sent, send2).wait()


def local(traces, aperture_lists, aperture_counts):
    bf16, f32 = jnp.bfloat16, jnp.float32
    dma = pltpu.SemaphoreType.DMA
    out = pl.pallas_call(
        kernel,
        out_shape=jax.ShapeDtypeStruct((FREQS, 2, TS, TR), f32),
        in_specs=[pl.BlockSpec(memory_space=pl.ANY)] * 4,
        out_specs=pl.BlockSpec(memory_space=pltpu.VMEM),
        scratch_shapes=[
            pltpu.VMEM((TS, TR, NT), bf16),
            pltpu.VMEM((128, NT), bf16),
            pltpu.SMEM((1, 1, APB), jnp.int32),
            pltpu.SMEM((1, 1), jnp.int32),
            pltpu.VMEM((FREQS * PITCH, 128), f32),
            pltpu.VMEM((FREQS, TS, 128), bf16),
            pltpu.VMEM((2, NY, NS * TS, 128), bf16),
            pltpu.VMEM((CHIPS, 1, 128), f32),
            pltpu.VMEM((CHIPS, 1024), f32),
            pltpu.VMEM((CHIPS, 16, 1024), bf16),
            pltpu.VMEM((NS * TS, 512), bf16),
            pltpu.VMEM((512, 128), bf16),
            pltpu.VMEM((NY, NS * TS, 128), f32),
            pltpu.VMEM((NY, NS * TS, 128), bf16),
            pltpu.VMEM((NY, NS, TS, 128), bf16),
            dma((CHUNKS,)),
            dma,
            dma((2,)),
            dma,
            dma((NY,)),
            dma((NY,)),
            dma((NY,)),
            dma,
            dma((NY,)),
            dma((9,)),
            dma((9,)),
        ],
        compiler_params=pltpu.CompilerParams(
            collective_id=0, has_side_effects=True, vmem_limit_bytes=int(VMEM_MIB * 2**20)
        ),
        cost_estimate=pl.CostEstimate(flops=2**30, bytes_accessed=8 * 2**20, transcendentals=0),
        name="multiples",
    )(traces, jnp.asarray(dft_table()), aperture_lists, aperture_counts)
    return out * SCALE


def solution(mesh):
    placed = (P("shot", "rcv", None), P("shot", "rcv", None), P("shot", "rcv"))
    return jax.shard_map(
        local, mesh=mesh, in_specs=placed, out_specs=P(None, None, "shot", "rcv"), check_vma=False
    )
```

```python
import math

import jax
import jax.numpy as jnp
import ml_dtypes
import numpy as np
from jax import lax
from jax.experimental import pallas as pl
from jax.experimental.pallas import tpu as pltpu
from jax.sharding import PartitionSpec as P

MESH = pl.DeviceIdType.MESH

NT = 1024
BAND = 32
APB = 8
FIRST = 32
SECOND = 128
FREQS = 64
TS = 32
TR = 64
NS = 16
NY = 4
CHIPS = 64
SCALE = 1.0 / math.sqrt(APB * TS)
CHUNKS = 2
PITCH = 40
VMEM_MIB = 60
BACK = (2, 1, 3, 0)
PLANE = [(a, b) for a in (2, 1, 3, 0) for b in (2, 1, 3, 0)]


def dft_table():
    sample = np.arange(NT)
    bins = np.concatenate([FIRST + np.arange(BAND), SECOND + np.arange(BAND)])
    phase = (bins[:, None] * sample[None, :] % NT).astype(np.float32) * np.float32(2.0 * math.pi / NT)
    phase = phase.astype(np.float64)
    factor = 1.0 / math.sqrt(NT)
    return (np.concatenate([np.cos(phase), -np.sin(phase)], axis=0) * factor).astype(np.float32).astype(
        ml_dtypes.bfloat16
    )


def kernel(
    traces,
    table_hbm,
    lists_hbm,
    back,
    tr,
    table,
    lists,
    specf,
    spec,
    grid,
    mtab,
    mrow,
    mask,
    masked,
    rhat,
    acc,
    prod,
    load_sem,
    table_sem,
    small_sem,
    send1,
    recv1,
    xsend,
    xrecv,
    send2,
    recv2,
    msend,
    mrecv,
    ready,
):
    shot = lax.axis_index("shot")
    rcv = lax.axis_index("rcv")
    y = rcv // 2
    core = rcv % 2
    z, x = shot // 4, shot % 4
    me = y * NS + shot
    sibling = (shot, y * 2 + 1 - core)
    zs = [(z + d) % 4 * 4 for d in range(4)]
    xs = [(x + d) % 4 for d in range(4)]
    ys = [(y + d) % 4 for d in range(4)]

    per = TS // CHUNKS
    loads = [
        pltpu.make_async_copy(traces.at[pl.ds(n * per, per)], tr.at[pl.ds(n * per, per)], load_sem.at[n])
        for n in range(CHUNKS)
    ]
    table_load = pltpu.make_async_copy(table_hbm, table, table_sem)
    lists_load = pltpu.make_async_copy(lists_hbm, lists, small_sem)
    table_load.start()
    for load in loads:
        load.start()
    lists_load.start()

    barrier = pltpu.get_barrier_semaphore()
    pl.semaphore_signal(barrier, inc=1, device_id=sibling, device_id_type=MESH)
    for d in (1, 2, 3):
        pl.semaphore_signal(barrier, inc=1, device_id=(zs[d] + x, rcv), device_id_type=MESH)
    for dx, dy in PLANE:
        if dx or dy:
            pl.semaphore_signal(
                barrier, inc=1, device_id=(z * 4 + xs[dx], ys[dy] * 2 + core), device_id_type=MESH
            )

    lists_load.wait()
    lane = lax.broadcasted_iota(jnp.int32, (1, 128), 1)
    member = jnp.where(lane == lists[0, 0, 0], 1.0, 0.0)
    for k in range(1, APB):
        entry = lists[0, 0, k]
        block = jnp.where(entry == 0, -1, entry)
        member = jnp.where(lane == block, 1.0, member)
    mrank = shot * NY + y
    mtab[mrank] = member

    low = lax.broadcasted_iota(jnp.int32, (FREQS, 128), 1) < TR
    table_load.wait()
    for n in range(CHUNKS):
        loads[n].wait()
        rows = tr[n * per : (n + 1) * per].reshape(per * TR, NT)
        flat = lax.dot_general(
            table[...], rows, (((1,), (1,)), ((), ())), preferred_element_type=jnp.float32
        )
        for p in range(per // 2):
            first = n * per + 2 * p
            re = flat[:FREQS, p * 128 : p * 128 + 128]
            im = flat[FREQS:, p * 128 : p * 128 + 128]
            specf[pl.ds(first, FREQS, stride=PITCH), :] = jnp.where(low, re, pltpu.roll(im, TR, 1))
            specf[pl.ds(first + 1, FREQS, stride=PITCH), :] = jnp.where(low, pltpu.roll(re, TR, 1), im)
    spec[...] = specf[...].reshape(FREQS, PITCH, 128)[:, :TS].astype(jnp.bfloat16)

    def mask_copy(d):
        return pltpu.make_async_remote_copy(
            src_ref=mtab.at[pl.ds(z * NS, NS)],
            dst_ref=mtab.at[pl.ds(z * NS, NS)],
            send_sem=msend.at[NS - 1 + d],
            recv_sem=mrecv.at[NS - 1 + d],
            device_id=(zs[d] + x, rcv),
            device_id_type=MESH,
        )

    def mask_start():
        for d in (1, 2, 3):
            mask_copy(d).start()

    def mask_wait():
        for d in (1, 2, 3):
            mask_copy(d).wait()

    def plane_copy(dx, dy):
        return pltpu.make_async_remote_copy(
            src_ref=mtab.at[pl.ds(mrank, 1)],
            dst_ref=mtab.at[pl.ds(mrank, 1)],
            send_sem=msend.at[dx * 4 + dy],
            recv_sem=mrecv.at[dx * 4 + dy],
            device_id=(z * 4 + xs[dx], ys[dy] * 2 + core),
            device_id_type=MESH,
        )

    def plane_start():
        for k in range(1, NS):
            plane_copy(k // 4, k % 4).start()

    def plane_wait():
        for k in range(1, NS):
            plane_copy(k // 4, k % 4).wait()

    mine = pl.ds(pl.multiple_of(shot * TS, TS), TS)

    def scatter(plane, dx, dy):
        ts = plane * 4 + xs[dx]
        pltpu.make_async_remote_copy(
            src_ref=spec.at[ys[dy] * NS + ts],
            dst_ref=grid.at[core, y, mine],
            send_sem=send1,
            recv_sem=recv1.at[y],
            device_id=(ts, ys[dy] * 2 + core),
            device_id_type=MESH,
        ).start()

    pl.semaphore_wait(barrier, NS + 3)
    for d in (1, 2, 3):
        pl.semaphore_signal(ready.at[z], inc=1, device_id=(zs[d] + x, rcv), device_id_type=MESH)
    plane_start()
    for dx, dy in PLANE:
        if dx or dy:
            scatter(z, dx, dy)
    pltpu.make_async_copy(spec.at[me], grid.at[core, y, mine], recv1.at[y]).start()
    for k in range(3):
        plane = (z + (2, 1, 3)[k]) % 4
        pl.semaphore_wait(ready.at[plane], 1)
        for dx, dy in PLANE:
            scatter(plane, dx, dy)
    plane_wait()
    mask_start()

    block = lax.broadcasted_iota(jnp.int32, (128, 1024), 0)
    column = lax.broadcasted_iota(jnp.int32, (128, 1024), 1)
    tile = column % 512 // 128 * 2 + (column // 512 + core) % 2
    expand = jnp.where(block == 2 * tile + column % TR // TS, 1.0, 0.0).astype(jnp.bfloat16)
    def slab_copy(ty):
        return pltpu.make_async_remote_copy(
            src_ref=grid.at[core, ty],
            dst_ref=grid.at[core, ty],
            send_sem=xsend.at[ty],
            recv_sem=xrecv.at[ty],
            device_id=sibling,
            device_id_type=MESH,
        )

    for d in (0, 3, 2, 1):
        slab = grid.at[core, ys[d]]
        pltpu.make_async_copy(slab, slab, recv1.at[ys[d]]).wait()
        slab_copy(ys[d]).start()

    mask_wait()
    mrow[...] = jnp.dot(
        mtab[...].reshape(CHIPS, 128).astype(jnp.bfloat16), expand, preferred_element_type=jnp.float32
    )

    def spread(t, carry):
        mask[t % NY, t // NY] = jnp.broadcast_to(mrow[pl.ds(t, 1), :], (16, 1024)).astype(jnp.bfloat16)
        return carry

    lax.fori_loop(0, CHIPS, spread, 0, unroll=4)

    left64 = lax.broadcasted_iota(jnp.int32, (TR, 128), 1) < TR

    def half(d, h):
        par = core if h == 0 else 1 - core
        for k in range(NY):
            cols = slice(k * 128, k * 128 + 128)
            left = grid[par, k].reshape(NS, 2, 16, 128)
            weights = mask[ys[d], :, :, h * 512 + k * 128 : h * 512 + k * 128 + 128]
            masked[:, cols] = (left * weights[:, None]).reshape(NS * TS, 128)
            first = pl.multiple_of((2 * k + par) * TR, TR)
            part = grid[core, ys[d], pl.ds(first, TR), :]
            turned = pltpu.roll(part.astype(jnp.float32), TR, 1)
            rhat[k * 128 : k * 128 + TR, :] = part
            rhat[k * 128 + TR : (k + 1) * 128, :] = jnp.where(left64, -turned, turned).astype(jnp.bfloat16)
        return jnp.dot(masked[...], rhat[...], preferred_element_type=jnp.float32)

    for d in range(NY):
        acc[d] = half(d, 0)
    for k in range(NY):
        other = grid.at[1 - core, k]
        pltpu.make_async_copy(other, other, xrecv.at[k]).wait()
    for d in BACK:
        ty = ys[d]
        prod[ty] = (acc[d] + half(d, 1)).astype(jnp.bfloat16)
        for dz, dx in PLANE:
            if d or dz or dx:
                ts = zs[dz] + xs[dx]
                pltpu.make_async_remote_copy(
                    src_ref=prod.at[ty, pl.ds(pl.multiple_of(ts * TS, TS), TS)],
                    dst_ref=back.at[y, shot],
                    send_sem=send2,
                    recv_sem=recv2.at[d],
                    device_id=(ts, ty * 2 + core),
                    device_id_type=MESH,
                ).start()
            else:
                pltpu.make_async_copy(prod.at[y, mine], back.at[y, shot], recv2.at[0]).start()

    for d in BACK:
        ty = ys[-d % 4]
        pltpu.make_async_copy(back.at[ty], back.at[ty], recv2.at[d]).wait()

    for k in range(NY):
        slab_copy(k).wait_send()
    sent = spec.at[pl.ds(0, CHIPS - 1)]
    pltpu.make_async_copy(sent, sent, send1).wait()
    pltpu.make_async_copy(sent, sent, send2).wait()


def widen(back, out, tiles, wide, in_sem, out_sem):
    loads = [pltpu.make_async_copy(back.at[k], tiles.at[k], in_sem.at[k]) for k in range(NY)]
    for load in loads:
        load.start()
    stores = []
    for k in range(NY):
        part = pl.ds(k * NS, NS)
        loads[k].wait()
        for n in range(NS):
            tile = tiles[k, n].astype(jnp.float32) * SCALE
            wide[k * NS + n, 0] = tile[:, :TR]
            wide[k * NS + n, 1] = pltpu.roll(tile, TR, 1)[:, :TR]
        stores.append(pltpu.make_async_copy(wide.at[part], out.at[part], out_sem.at[k]))
        stores[k].start()
    for store in stores:
        store.wait()


def local(traces, aperture_lists, aperture_counts):
    bf16, f32 = jnp.bfloat16, jnp.float32
    dma = pltpu.SemaphoreType.DMA
    back = pl.pallas_call(
        kernel,
        out_shape=jax.ShapeDtypeStruct((NY, NS, TS, 128), bf16),
        in_specs=[pl.BlockSpec(memory_space=pl.ANY)] * 3,
        out_specs=pl.BlockSpec(memory_space=pl.ANY),
        scratch_shapes=[
            pltpu.VMEM((TS, TR, NT), bf16),
            pltpu.VMEM((128, NT), bf16),
            pltpu.SMEM((1, 1, APB), jnp.int32),
            pltpu.VMEM((FREQS * PITCH, 128), f32),
            pltpu.VMEM((FREQS, TS, 128), bf16),
            pltpu.VMEM((2, NY, NS * TS, 128), bf16),
            pltpu.VMEM((CHIPS, 1, 128), f32),
            pltpu.VMEM((CHIPS, 1024), f32),
            pltpu.VMEM((NY, NS, 16, 1024), bf16),
            pltpu.VMEM((NS * TS, 512), bf16),
            pltpu.VMEM((512, 128), bf16),
            pltpu.VMEM((NY, NS * TS, 128), f32),
            pltpu.VMEM((NY, NS * TS, 128), bf16),
            dma((CHUNKS,)),
            dma,
            dma,
            dma,
            dma((NY,)),
            dma((NY,)),
            dma((NY,)),
            dma,
            dma((NY,)),
            dma((19,)),
            dma((19,)),
            pltpu.SemaphoreType.REGULAR((4,)),
        ],
        compiler_params=pltpu.CompilerParams(
            collective_id=0, has_side_effects=True, vmem_limit_bytes=int(VMEM_MIB * 2**20)
        ),
        cost_estimate=pl.CostEstimate(flops=2**30, bytes_accessed=8 * 2**20, transcendentals=0),
        name="multiples",
    )(traces, jnp.asarray(dft_table()), aperture_lists)
    return pl.pallas_call(
        widen,
        out_shape=jax.ShapeDtypeStruct((FREQS, 2, TS, TR), f32),
        in_specs=[pl.BlockSpec(memory_space=pl.ANY)],
        out_specs=pl.BlockSpec(memory_space=pl.ANY),
        scratch_shapes=[
            pltpu.VMEM((NY, NS, TS, 128), bf16),
            pltpu.VMEM((FREQS, 2, TS, TR), f32),
            dma((NY,)),
            dma((NY,)),
        ],
        compiler_params=pltpu.CompilerParams(vmem_limit_bytes=int(VMEM_MIB * 2**20)),
        cost_estimate=pl.CostEstimate(flops=2**20, bytes_accessed=3 * 2**20, transcendentals=0),
        name="widen",
    )(back)


def solution(mesh):
    placed = (P("shot", "rcv", None), P("shot", "rcv", None), P("shot", "rcv"))
    return jax.shard_map(
        local, mesh=mesh, in_specs=placed, out_specs=P(None, None, "shot", "rcv"), check_vma=False
    )
```

```python
import math

import jax
import jax.numpy as jnp
import ml_dtypes
import numpy as np
from jax import lax
from jax.experimental import pallas as pl
from jax.experimental.pallas import tpu as pltpu
from jax.sharding import PartitionSpec as P

MESH = pl.DeviceIdType.MESH

NT = 1024
BAND = 32
APB = 8
FIRST = 32
SECOND = 128
FREQS = 64
TS = 32
TR = 64
NS = 16
NY = 4
CHIPS = 64
SCALE = 1.0 / math.sqrt(APB * TS)
CHUNKS = 2
PITCH = 40
VMEM_MIB = 60
BACK = (2, 1, 3, 0)
PLANE = [(a, b) for a in (2, 1, 3, 0) for b in (2, 1, 3, 0)]


def dft_table():
    sample = np.arange(NT)
    bins = np.concatenate([FIRST + np.arange(BAND), SECOND + np.arange(BAND)])
    phase = (bins[:, None] * sample[None, :] % NT).astype(np.float32) * np.float32(2.0 * math.pi / NT)
    phase = phase.astype(np.float64)
    factor = 1.0 / math.sqrt(NT)
    return (np.concatenate([np.cos(phase), -np.sin(phase)], axis=0) * factor).astype(np.float32).astype(
        ml_dtypes.bfloat16
    )


def kernel(
    traces,
    table_hbm,
    lists_hbm,
    back,
    tr,
    table,
    lists,
    specf,
    spec,
    grid,
    mtab,
    mrow,
    mask,
    masked,
    rhat,
    acc,
    prod,
    load_sem,
    table_sem,
    small_sem,
    send1,
    recv1,
    xsend,
    xrecv,
    send2,
    recv2,
    msend,
    mrecv,
    ready,
):
    shot = lax.axis_index("shot")
    rcv = lax.axis_index("rcv")
    y = rcv // 2
    core = rcv % 2
    z, x = shot // 4, shot % 4
    me = y * NS + shot
    sibling = (shot, y * 2 + 1 - core)
    zs = [(z + d) % 4 * 4 for d in range(4)]
    xs = [(x + d) % 4 for d in range(4)]
    ys = [(y + d) % 4 for d in range(4)]

    per = TS // CHUNKS
    loads = [
        pltpu.make_async_copy(traces.at[pl.ds(n * per, per)], tr.at[pl.ds(n * per, per)], load_sem.at[n])
        for n in range(CHUNKS)
    ]
    table_load = pltpu.make_async_copy(table_hbm, table, table_sem)
    lists_load = pltpu.make_async_copy(lists_hbm, lists, small_sem)
    table_load.start()
    for load in loads:
        load.start()
    lists_load.start()

    barrier = pltpu.get_barrier_semaphore()
    pl.semaphore_signal(barrier, inc=1, device_id=sibling, device_id_type=MESH)
    for d in (1, 2, 3):
        pl.semaphore_signal(
            barrier, inc=1, device_id=(shot, ys[d] * 2 + core), device_id_type=MESH
        )
    for dz, dx in PLANE:
        if dz or dx:
            pl.semaphore_signal(
                barrier, inc=1, device_id=(zs[dz] + xs[dx], rcv), device_id_type=MESH
            )

    lists_load.wait()
    lane = lax.broadcasted_iota(jnp.int32, (1, 128), 1)
    member = jnp.where(lane == lists[0, 0, 0], 1.0, 0.0)
    for k in range(1, APB):
        entry = lists[0, 0, k]
        block = jnp.where(entry == 0, -1, entry)
        member = jnp.where(lane == block, 1.0, member)
    mtab[me] = member

    low = lax.broadcasted_iota(jnp.int32, (FREQS, 128), 1) < TR
    table_load.wait()
    for n in range(CHUNKS):
        loads[n].wait()
        rows = tr[n * per : (n + 1) * per].reshape(per * TR, NT)
        flat = lax.dot_general(
            table[...], rows, (((1,), (1,)), ((), ())), preferred_element_type=jnp.float32
        )
        for p in range(per // 2):
            first = n * per + 2 * p
            re = flat[:FREQS, p * 128 : p * 128 + 128]
            im = flat[FREQS:, p * 128 : p * 128 + 128]
            specf[pl.ds(first, FREQS, stride=PITCH), :] = jnp.where(low, re, pltpu.roll(im, TR, 1))
            specf[pl.ds(first + 1, FREQS, stride=PITCH), :] = jnp.where(low, pltpu.roll(re, TR, 1), im)
    spec[...] = specf[...].reshape(FREQS, PITCH, 128)[:, :TS].astype(jnp.bfloat16)

    def mask_copy(stage, d):
        if stage == 0:
            rows, to = pl.ds(me, 1), (zs[0] + xs[d], rcv)
        elif stage == 1:
            rows, to = pl.ds(y * NS + z * 4, 4), (zs[d] + x, rcv)
        else:
            rows, to = pl.ds(y * NS, NS), (shot, ys[d] * 2 + core)
        return pltpu.make_async_remote_copy(
            src_ref=mtab.at[rows],
            dst_ref=mtab.at[rows],
            send_sem=msend.at[stage * 3 + d - 1],
            recv_sem=mrecv.at[stage * 3 + d - 1],
            device_id=to,
            device_id_type=MESH,
        )

    def mask_start(stage):
        for d in (1, 2, 3):
            mask_copy(stage, d).start()

    def mask_wait(stage):
        for d in (1, 2, 3):
            mask_copy(stage, d).wait()

    mine = pl.ds(pl.multiple_of(shot * TS, TS), TS)

    def scatter(plane, dz, dx):
        ts = zs[dz] + xs[dx]
        pltpu.make_async_remote_copy(
            src_ref=spec.at[plane * NS + ts],
            dst_ref=grid.at[core, y, mine],
            send_sem=send1,
            recv_sem=recv1.at[y],
            device_id=(ts, plane * 2 + core),
            device_id_type=MESH,
        ).start()

    pl.semaphore_wait(barrier, NS + 3)
    for d in (1, 2, 3):
        pl.semaphore_signal(ready.at[y], inc=1, device_id=(shot, ys[d] * 2 + core), device_id_type=MESH)
    mask_start(0)
    for dz, dx in PLANE:
        if dz or dx:
            scatter(y, dz, dx)
    pltpu.make_async_copy(spec.at[me], grid.at[core, y, mine], recv1.at[y]).start()
    for d in (2, 1, 3):
        pl.semaphore_wait(ready.at[ys[d]], 1)
        for dz, dx in PLANE:
            scatter(ys[d], dz, dx)
    mask_wait(0)
    mask_start(1)
    mask_wait(1)
    mask_start(2)

    block = lax.broadcasted_iota(jnp.int32, (128, 1024), 0)
    column = lax.broadcasted_iota(jnp.int32, (128, 1024), 1)
    tile = column % 512 // 128 * 2 + (column // 512 + core) % 2
    expand = jnp.where(block == 2 * tile + column % TR // TS, 1.0, 0.0).astype(jnp.bfloat16)
    def slab_copy(ty):
        return pltpu.make_async_remote_copy(
            src_ref=grid.at[core, ty],
            dst_ref=grid.at[core, ty],
            send_sem=xsend.at[ty],
            recv_sem=xrecv.at[ty],
            device_id=sibling,
            device_id_type=MESH,
        )

    for d in (0, 2, 3, 1):
        slab = grid.at[core, ys[d]]
        pltpu.make_async_copy(slab, slab, recv1.at[ys[d]]).wait()
        slab_copy(ys[d]).start()

    mask_wait(2)
    mrow[...] = jnp.dot(
        mtab[...].reshape(CHIPS, 128).astype(jnp.bfloat16), expand, preferred_element_type=jnp.float32
    )

    def spread(t, carry):
        mask[t // NS, t % NS] = jnp.broadcast_to(mrow[pl.ds(t, 1), :], (16, 1024)).astype(jnp.bfloat16)
        return carry

    lax.fori_loop(0, CHIPS, spread, 0, unroll=4)

    left64 = lax.broadcasted_iota(jnp.int32, (TR, 128), 1) < TR

    def half(d, h):
        par = core if h == 0 else 1 - core
        for k in range(NY):
            cols = slice(k * 128, k * 128 + 128)
            left = grid[par, k].reshape(NS, 2, 16, 128)
            weights = mask[ys[d], :, :, h * 512 + k * 128 : h * 512 + k * 128 + 128]
            masked[:, cols] = (left * weights[:, None]).reshape(NS * TS, 128)
            first = pl.multiple_of((2 * k + par) * TR, TR)
            part = grid[core, ys[d], pl.ds(first, TR), :]
            turned = pltpu.roll(part.astype(jnp.float32), TR, 1)
            rhat[k * 128 : k * 128 + TR, :] = part
            rhat[k * 128 + TR : (k + 1) * 128, :] = jnp.where(left64, -turned, turned).astype(jnp.bfloat16)
        return jnp.dot(masked[...], rhat[...], preferred_element_type=jnp.float32)

    for d in range(NY):
        acc[d] = half(d, 0)
    for k in range(NY):
        other = grid.at[1 - core, k]
        pltpu.make_async_copy(other, other, xrecv.at[k]).wait()
    for d in BACK:
        ty = ys[d]
        prod[ty] = (acc[d] + half(d, 1)).astype(jnp.bfloat16)
        for dz, dx in [(a, b) for a in range(4) for b in (2, 1, 3, 0)]:
            ts = dz * 4 + xs[dx]

            @pl.when(jnp.logical_or(ts != shot, ty != y))
            def _():
                pltpu.make_async_remote_copy(
                    src_ref=prod.at[ty, pl.ds(pl.multiple_of(ts * TS, TS), TS)],
                    dst_ref=back.at[y, shot],
                    send_sem=send2,
                    recv_sem=recv2,
                    device_id=(ts, ty * 2 + core),
                    device_id_type=MESH,
                ).start()

    pltpu.make_async_copy(prod.at[y, mine], back.at[y, shot], recv2).start()
    pltpu.make_async_copy(back, back, recv2).wait()
    for k in range(NY):
        slab_copy(k).wait_send()
    sent = spec.at[pl.ds(0, CHIPS - 1)]
    pltpu.make_async_copy(sent, sent, send1).wait()
    pltpu.make_async_copy(sent, sent, send2).wait()


def widen(back, out, tiles, wide, in_sem, out_sem):
    loads = [pltpu.make_async_copy(back.at[k], tiles.at[k], in_sem.at[k]) for k in range(NY)]
    for load in loads:
        load.start()
    stores = []
    for k in range(NY):
        part = pl.ds(k * NS, NS)
        loads[k].wait()
        for n in range(NS):
            tile = tiles[k, n].astype(jnp.float32) * SCALE
            wide[k * NS + n, 0] = tile[:, :TR]
            wide[k * NS + n, 1] = pltpu.roll(tile, TR, 1)[:, :TR]
        stores.append(pltpu.make_async_copy(wide.at[part], out.at[part], out_sem.at[k]))
        stores[k].start()
    for store in stores:
        store.wait()


def local(traces, aperture_lists, aperture_counts):
    bf16, f32 = jnp.bfloat16, jnp.float32
    dma = pltpu.SemaphoreType.DMA
    back = pl.pallas_call(
        kernel,
        out_shape=jax.ShapeDtypeStruct((NY, NS, TS, 128), bf16),
        in_specs=[pl.BlockSpec(memory_space=pl.ANY)] * 3,
        out_specs=pl.BlockSpec(memory_space=pl.ANY),
        scratch_shapes=[
            pltpu.VMEM((TS, TR, NT), bf16),
            pltpu.VMEM((128, NT), bf16),
            pltpu.SMEM((1, 1, APB), jnp.int32),
            pltpu.VMEM((FREQS * PITCH, 128), f32),
            pltpu.VMEM((FREQS, TS, 128), bf16),
            pltpu.VMEM((2, NY, NS * TS, 128), bf16),
            pltpu.VMEM((CHIPS, 1, 128), f32),
            pltpu.VMEM((CHIPS, 1024), f32),
            pltpu.VMEM((NY, NS, 16, 1024), bf16),
            pltpu.VMEM((NS * TS, 512), bf16),
            pltpu.VMEM((512, 128), bf16),
            pltpu.VMEM((NY, NS * TS, 128), f32),
            pltpu.VMEM((NY, NS * TS, 128), bf16),
            dma((CHUNKS,)),
            dma,
            dma,
            dma,
            dma((NY,)),
            dma((NY,)),
            dma((NY,)),
            dma,
            dma,
            dma((9,)),
            dma((9,)),
            pltpu.SemaphoreType.REGULAR((4,)),
        ],
        compiler_params=pltpu.CompilerParams(
            collective_id=0, has_side_effects=True, vmem_limit_bytes=int(VMEM_MIB * 2**20)
        ),
        cost_estimate=pl.CostEstimate(flops=2**30, bytes_accessed=8 * 2**20, transcendentals=0),
        name="multiples",
    )(traces, jnp.asarray(dft_table()), aperture_lists)
    return pl.pallas_call(
        widen,
        out_shape=jax.ShapeDtypeStruct((FREQS, 2, TS, TR), f32),
        in_specs=[pl.BlockSpec(memory_space=pl.ANY)],
        out_specs=pl.BlockSpec(memory_space=pl.ANY),
        scratch_shapes=[
            pltpu.VMEM((NY, NS, TS, 128), bf16),
            pltpu.VMEM((FREQS, 2, TS, TR), f32),
            dma((NY,)),
            dma((NY,)),
        ],
        compiler_params=pltpu.CompilerParams(vmem_limit_bytes=int(VMEM_MIB * 2**20)),
        cost_estimate=pl.CostEstimate(flops=2**20, bytes_accessed=3 * 2**20, transcendentals=0),
        name="widen",
    )(back)


def solution(mesh):
    placed = (P("shot", "rcv", None), P("shot", "rcv", None), P("shot", "rcv"))
    return jax.shard_map(
        local, mesh=mesh, in_specs=placed, out_specs=P(None, None, "shot", "rcv"), check_vma=False
    )
```

```python
import math

import jax
import jax.numpy as jnp
import ml_dtypes
import numpy as np
from jax import lax
from jax.experimental import pallas as pl
from jax.experimental.pallas import tpu as pltpu
from jax.sharding import PartitionSpec as P

MESH = pl.DeviceIdType.MESH

NT = 1024
BAND = 32
APB = 8
FIRST = 32
SECOND = 128
FREQS = 64
TS = 32
TR = 64
NS = 16
NY = 4
CHIPS = 64
SCALE = 1.0 / math.sqrt(APB * TS)
CHUNKS = 2
PITCH = 40
VMEM_MIB = 60
BACK = (2, 1, 3, 0)
PLANE = [(a, b) for a in (2, 1, 3, 0) for b in (2, 1, 3, 0)]


def dft_table():
    sample = np.arange(NT)
    bins = np.concatenate([FIRST + np.arange(BAND), SECOND + np.arange(BAND)])
    phase = (bins[:, None] * sample[None, :] % NT).astype(np.float32) * np.float32(2.0 * math.pi / NT)
    phase = phase.astype(np.float64)
    factor = 1.0 / math.sqrt(NT)
    return (np.concatenate([np.cos(phase), -np.sin(phase)], axis=0) * factor).astype(np.float32).astype(
        ml_dtypes.bfloat16
    )


def kernel(
    traces,
    table_hbm,
    lists_hbm,
    back,
    tr,
    table,
    lists,
    specf,
    spec,
    grid,
    mtab,
    mrow,
    mask,
    masked,
    rhat,
    acc,
    prod,
    load_sem,
    table_sem,
    small_sem,
    send1,
    recv1,
    xsend,
    xrecv,
    send2,
    recv2,
    msend,
    mrecv,
    ready,
):
    shot = lax.axis_index("shot")
    rcv = lax.axis_index("rcv")
    y = rcv // 2
    core = rcv % 2
    z, x = shot // 4, shot % 4
    me = y * NS + shot
    sibling = (shot, y * 2 + 1 - core)
    zs = [(z + d) % 4 * 4 for d in range(4)]
    xs = [(x + d) % 4 for d in range(4)]
    ys = [(y + d) % 4 for d in range(4)]

    per = TS // CHUNKS
    loads = [
        pltpu.make_async_copy(traces.at[pl.ds(n * per, per)], tr.at[pl.ds(n * per, per)], load_sem.at[n])
        for n in range(CHUNKS)
    ]
    table_load = pltpu.make_async_copy(table_hbm, table, table_sem)
    lists_load = pltpu.make_async_copy(lists_hbm, lists, small_sem)
    table_load.start()
    for load in loads:
        load.start()
    lists_load.start()

    barrier = pltpu.get_barrier_semaphore()
    pl.semaphore_signal(barrier, inc=1, device_id=sibling, device_id_type=MESH)
    for d in (1, 2, 3):
        pl.semaphore_signal(
            barrier, inc=1, device_id=(shot, ys[d] * 2 + core), device_id_type=MESH
        )
    for dz, dx in PLANE:
        if dz or dx:
            pl.semaphore_signal(
                barrier, inc=1, device_id=(zs[dz] + xs[dx], rcv), device_id_type=MESH
            )

    lists_load.wait()
    lane = lax.broadcasted_iota(jnp.int32, (1, 128), 1)
    member = jnp.where(lane == lists[0, 0, 0], 1.0, 0.0)
    for k in range(1, APB):
        entry = lists[0, 0, k]
        block = jnp.where(entry == 0, -1, entry)
        member = jnp.where(lane == block, 1.0, member)
    mtab[me] = member

    low = lax.broadcasted_iota(jnp.int32, (FREQS, 128), 1) < TR
    table_load.wait()
    for n in range(CHUNKS):
        loads[n].wait()
        rows = tr[n * per : (n + 1) * per].reshape(per * TR, NT)
        flat = lax.dot_general(
            table[...], rows, (((1,), (1,)), ((), ())), preferred_element_type=jnp.float32
        )
        for p in range(per // 2):
            first = n * per + 2 * p
            re = flat[:FREQS, p * 128 : p * 128 + 128]
            im = flat[FREQS:, p * 128 : p * 128 + 128]
            specf[pl.ds(first, FREQS, stride=PITCH), :] = jnp.where(low, re, pltpu.roll(im, TR, 1))
            specf[pl.ds(first + 1, FREQS, stride=PITCH), :] = jnp.where(low, pltpu.roll(re, TR, 1), im)
    spec[...] = specf[...].reshape(FREQS, PITCH, 128)[:, :TS].astype(jnp.bfloat16)

    def mask_copy(stage, d):
        if stage == 0:
            rows, to = pl.ds(me, 1), (zs[0] + xs[d], rcv)
        elif stage == 1:
            rows, to = pl.ds(y * NS + z * 4, 4), (zs[d] + x, rcv)
        else:
            rows, to = pl.ds(y * NS, NS), (shot, ys[d] * 2 + core)
        return pltpu.make_async_remote_copy(
            src_ref=mtab.at[rows],
            dst_ref=mtab.at[rows],
            send_sem=msend.at[stage * 3 + d - 1],
            recv_sem=mrecv.at[stage * 3 + d - 1],
            device_id=to,
            device_id_type=MESH,
        )

    def mask_start(stage):
        for d in (1, 2, 3):
            mask_copy(stage, d).start()

    def mask_wait(stage):
        for d in (1, 2, 3):
            mask_copy(stage, d).wait()

    mine = pl.ds(pl.multiple_of(shot * TS, TS), TS)

    def scatter(plane, dz, dx):
        ts = zs[dz] + xs[dx]
        pltpu.make_async_remote_copy(
            src_ref=spec.at[plane * NS + ts],
            dst_ref=grid.at[core, y, mine],
            send_sem=send1,
            recv_sem=recv1.at[y],
            device_id=(ts, plane * 2 + core),
            device_id_type=MESH,
        ).start()

    pl.semaphore_wait(barrier, NS + 3)
    for d in (1, 2, 3):
        pl.semaphore_signal(ready.at[y], inc=1, device_id=(shot, ys[d] * 2 + core), device_id_type=MESH)
    mask_start(0)
    for dz, dx in PLANE:
        if dz or dx:
            scatter(y, dz, dx)
    pltpu.make_async_copy(spec.at[me], grid.at[core, y, mine], recv1.at[y]).start()
    for d in (2, 1, 3):
        pl.semaphore_wait(ready.at[ys[d]], 1)
        for dz, dx in PLANE:
            scatter(ys[d], dz, dx)
    mask_wait(0)
    mask_start(1)
    mask_wait(1)
    mask_start(2)

    block = lax.broadcasted_iota(jnp.int32, (128, 1024), 0)
    column = lax.broadcasted_iota(jnp.int32, (128, 1024), 1)
    tile = column % 512 // 128 * 2 + (column // 512 + core) % 2
    expand = jnp.where(block == 2 * tile + column % TR // TS, 1.0, 0.0).astype(jnp.bfloat16)
    def slab_copy(ty):
        return pltpu.make_async_remote_copy(
            src_ref=grid.at[core, ty],
            dst_ref=grid.at[core, ty],
            send_sem=xsend.at[ty],
            recv_sem=xrecv.at[ty],
            device_id=sibling,
            device_id_type=MESH,
        )

    for d in (0, 2, 3, 1):
        slab = grid.at[core, ys[d]]
        pltpu.make_async_copy(slab, slab, recv1.at[ys[d]]).wait()
        slab_copy(ys[d]).start()

    mask_wait(2)
    mrow[...] = jnp.dot(
        mtab[...].reshape(CHIPS, 128).astype(jnp.bfloat16), expand, preferred_element_type=jnp.float32
    )

    def spread(t, carry):
        mask[t // NS, t % NS] = jnp.broadcast_to(mrow[pl.ds(t, 1), :], (16, 1024)).astype(jnp.bfloat16)
        return carry

    lax.fori_loop(0, CHIPS, spread, 0, unroll=4)

    left64 = lax.broadcasted_iota(jnp.int32, (TR, 128), 1) < TR

    def part(d, h, slabs):
        par = core if h == 0 else 1 - core
        width = len(slabs) * 128
        for n, ds in enumerate(slabs):
            k = ys[ds]
            left = grid[par, k].reshape(NS, 2, 16, 128)
            weights = mask[ys[d], :, :, pl.ds(pl.multiple_of(h * 512 + k * 128, 128), 128)]
            masked[:, n * 128 : n * 128 + 128] = (left * weights[:, None]).reshape(NS * TS, 128)
            first = pl.multiple_of((2 * k + par) * TR, TR)
            right = grid[core, ys[d], pl.ds(first, TR), :]
            turned = pltpu.roll(right.astype(jnp.float32), TR, 1)
            rhat[n * 128 : n * 128 + TR, :] = right
            rhat[n * 128 + TR : (n + 1) * 128, :] = jnp.where(left64, -turned, turned).astype(jnp.bfloat16)
        return jnp.dot(masked[:, :width], rhat[:width, :], preferred_element_type=jnp.float32)

    def other_slab(ds):
        slab = grid.at[1 - core, ys[ds]]
        pltpu.make_async_copy(slab, slab, xrecv.at[ys[ds]]).wait()

    for d in range(NY):
        acc[d] = part(d, 0, (0, 2, 3, 1))
    other_slab(0)
    other_slab(2)
    for d in range(NY):
        acc[d] += part(d, 1, (0, 2))
    other_slab(3)
    other_slab(1)
    for d in BACK:
        ty = ys[d]
        prod[ty] = (acc[d] + part(d, 1, (3, 1))).astype(jnp.bfloat16)
        for dz, dx in [(a, b) for a in range(4) for b in (2, 1, 3, 0)]:
            ts = dz * 4 + xs[dx]

            @pl.when(jnp.logical_or(ts != shot, ty != y))
            def _():
                pltpu.make_async_remote_copy(
                    src_ref=prod.at[ty, pl.ds(pl.multiple_of(ts * TS, TS), TS)],
                    dst_ref=back.at[y, shot],
                    send_sem=send2,
                    recv_sem=recv2,
                    device_id=(ts, ty * 2 + core),
                    device_id_type=MESH,
                ).start()

    pltpu.make_async_copy(prod.at[y, mine], back.at[y, shot], recv2).start()
    pltpu.make_async_copy(back, back, recv2).wait()
    for k in range(NY):
        slab_copy(k).wait_send()
    sent = spec.at[pl.ds(0, CHIPS - 1)]
    pltpu.make_async_copy(sent, sent, send1).wait()
    pltpu.make_async_copy(sent, sent, send2).wait()


def widen(back, out, tiles, wide, in_sem, out_sem):
    loads = [pltpu.make_async_copy(back.at[k], tiles.at[k], in_sem.at[k]) for k in range(NY)]
    for load in loads:
        load.start()
    stores = []
    for k in range(NY):
        part = pl.ds(k * NS, NS)
        loads[k].wait()
        for n in range(NS):
            tile = tiles[k, n].astype(jnp.float32) * SCALE
            wide[k * NS + n, 0] = tile[:, :TR]
            wide[k * NS + n, 1] = pltpu.roll(tile, TR, 1)[:, :TR]
        stores.append(pltpu.make_async_copy(wide.at[part], out.at[part], out_sem.at[k]))
        stores[k].start()
    for store in stores:
        store.wait()


def local(traces, aperture_lists, aperture_counts):
    bf16, f32 = jnp.bfloat16, jnp.float32
    dma = pltpu.SemaphoreType.DMA
    back = pl.pallas_call(
        kernel,
        out_shape=jax.ShapeDtypeStruct((NY, NS, TS, 128), bf16),
        in_specs=[pl.BlockSpec(memory_space=pl.ANY)] * 3,
        out_specs=pl.BlockSpec(memory_space=pl.ANY),
        scratch_shapes=[
            pltpu.VMEM((TS, TR, NT), bf16),
            pltpu.VMEM((128, NT), bf16),
            pltpu.SMEM((1, 1, APB), jnp.int32),
            pltpu.VMEM((FREQS * PITCH, 128), f32),
            pltpu.VMEM((FREQS, TS, 128), bf16),
            pltpu.VMEM((2, NY, NS * TS, 128), bf16),
            pltpu.VMEM((CHIPS, 1, 128), f32),
            pltpu.VMEM((CHIPS, 1024), f32),
            pltpu.VMEM((NY, NS, 16, 1024), bf16),
            pltpu.VMEM((NS * TS, 512), bf16),
            pltpu.VMEM((512, 128), bf16),
            pltpu.VMEM((NY, NS * TS, 128), f32),
            pltpu.VMEM((NY, NS * TS, 128), bf16),
            dma((CHUNKS,)),
            dma,
            dma,
            dma,
            dma((NY,)),
            dma((NY,)),
            dma((NY,)),
            dma,
            dma,
            dma((9,)),
            dma((9,)),
            pltpu.SemaphoreType.REGULAR((4,)),
        ],
        compiler_params=pltpu.CompilerParams(
            collective_id=0, has_side_effects=True, vmem_limit_bytes=int(VMEM_MIB * 2**20)
        ),
        cost_estimate=pl.CostEstimate(flops=2**30, bytes_accessed=8 * 2**20, transcendentals=0),
        name="multiples",
    )(traces, jnp.asarray(dft_table()), aperture_lists)
    return pl.pallas_call(
        widen,
        out_shape=jax.ShapeDtypeStruct((FREQS, 2, TS, TR), f32),
        in_specs=[pl.BlockSpec(memory_space=pl.ANY)],
        out_specs=pl.BlockSpec(memory_space=pl.ANY),
        scratch_shapes=[
            pltpu.VMEM((NY, NS, TS, 128), bf16),
            pltpu.VMEM((FREQS, 2, TS, TR), f32),
            dma((NY,)),
            dma((NY,)),
        ],
        compiler_params=pltpu.CompilerParams(vmem_limit_bytes=int(VMEM_MIB * 2**20)),
        cost_estimate=pl.CostEstimate(flops=2**20, bytes_accessed=3 * 2**20, transcendentals=0),
        name="widen",
    )(back)


def solution(mesh):
    placed = (P("shot", "rcv", None), P("shot", "rcv", None), P("shot", "rcv"))
    return jax.shard_map(
        local, mesh=mesh, in_specs=placed, out_specs=P(None, None, "shot", "rcv"), check_vma=False
    )
```

```python
import math

import jax
import jax.numpy as jnp
import ml_dtypes
import numpy as np
from jax import lax
from jax.experimental import pallas as pl
from jax.experimental.pallas import tpu as pltpu
from jax.sharding import PartitionSpec as P

LOGICAL = pl.DeviceIdType.LOGICAL

NT = 1024
BAND = 32
APB = 8
FIRST = 32
SECOND = 128
FREQS = 64
TS = 32
TR = 64
NS = 16
NY = 4
CHIPS = 64
SCALE = 1.0 / math.sqrt(APB * TS)
CHUNKS = 2
PITCH = 40
VMEM_MIB = 60
BACK = (2, 1, 3, 0)
PLANE = [(a, b) for a in (2, 1, 3, 0) for b in (2, 1, 3, 0)]


def dft_table():
    sample = np.arange(NT)
    bins = np.concatenate([FIRST + np.arange(BAND), SECOND + np.arange(BAND)])
    phase = (bins[:, None] * sample[None, :] % NT).astype(np.float32) * np.float32(2.0 * math.pi / NT)
    phase = phase.astype(np.float64)
    factor = 1.0 / math.sqrt(NT)
    return (np.concatenate([np.cos(phase), -np.sin(phase)], axis=0) * factor).astype(np.float32).astype(
        ml_dtypes.bfloat16
    )


def kernel(
    traces,
    table_hbm,
    lists_hbm,
    back,
    tr,
    table,
    lists,
    specf,
    spec,
    grid,
    mtab,
    mrow,
    mask,
    masked,
    rhat,
    acc,
    prod,
    load_sem,
    table_sem,
    small_sem,
    send1,
    recv1,
    xsend,
    xrecv,
    send2,
    recv2,
    msend,
    mrecv,
    ready,
):
    shot = lax.axis_index("shot")
    rcv = lax.axis_index("rcv")
    y = rcv // 2
    core = rcv % 2
    z, x = shot // 4, shot % 4
    me = y * NS + shot
    sibling = shot * 8 + y * 2 + 1 - core
    zs = [(z + d) % 4 * 4 for d in range(4)]
    xs = [(x + d) % 4 for d in range(4)]
    ys = [(y + d) % 4 for d in range(4)]

    per = TS // CHUNKS
    loads = [
        pltpu.make_async_copy(traces.at[pl.ds(n * per, per)], tr.at[pl.ds(n * per, per)], load_sem.at[n])
        for n in range(CHUNKS)
    ]
    table_load = pltpu.make_async_copy(table_hbm, table, table_sem)
    lists_load = pltpu.make_async_copy(lists_hbm, lists, small_sem)
    table_load.start()
    for load in loads:
        load.start()
    lists_load.start()

    barrier = pltpu.get_barrier_semaphore()
    pl.semaphore_signal(barrier, inc=1, device_id=sibling, device_id_type=LOGICAL)
    for d in (1, 2, 3):
        pl.semaphore_signal(
            barrier, inc=1, device_id=shot * 8 + ys[d] * 2 + core, device_id_type=LOGICAL
        )
    for dz, dx in PLANE:
        if dz or dx:
            pl.semaphore_signal(
                barrier, inc=1, device_id=(zs[dz] + xs[dx]) * 8 + rcv, device_id_type=LOGICAL
            )

    lists_load.wait()
    lane = lax.broadcasted_iota(jnp.int32, (1, 128), 1)
    member = jnp.where(lane == lists[0, 0, 0], 1.0, 0.0)
    for k in range(1, APB):
        entry = lists[0, 0, k]
        block = jnp.where(entry == 0, -1, entry)
        member = jnp.where(lane == block, 1.0, member)
    mtab[me] = member

    low = lax.broadcasted_iota(jnp.int32, (FREQS, 128), 1) < TR
    table_load.wait()
    for n in range(CHUNKS):
        loads[n].wait()
        rows = tr[n * per : (n + 1) * per].reshape(per * TR, NT)
        flat = lax.dot_general(
            table[...], rows, (((1,), (1,)), ((), ())), preferred_element_type=jnp.float32
        )
        for p in range(per // 2):
            first = n * per + 2 * p
            re = flat[:FREQS, p * 128 : p * 128 + 128]
            im = flat[FREQS:, p * 128 : p * 128 + 128]
            specf[pl.ds(first, FREQS, stride=PITCH), :] = jnp.where(low, re, pltpu.roll(im, TR, 1))
            specf[pl.ds(first + 1, FREQS, stride=PITCH), :] = jnp.where(low, pltpu.roll(re, TR, 1), im)
    spec[...] = specf[...].reshape(FREQS, PITCH, 128)[:, :TS].astype(jnp.bfloat16)

    def mask_copy(stage, d):
        if stage == 0:
            rows, to = pl.ds(me, 1), (zs[0] + xs[d], rcv)
        elif stage == 1:
            rows, to = pl.ds(y * NS + z * 4, 4), (zs[d] + x, rcv)
        else:
            rows, to = pl.ds(y * NS, NS), (shot, ys[d] * 2 + core)
        return pltpu.make_async_remote_copy(
            src_ref=mtab.at[rows],
            dst_ref=mtab.at[rows],
            send_sem=msend.at[stage * 3 + d - 1],
            recv_sem=mrecv.at[stage * 3 + d - 1],
            device_id=to[0] * 8 + to[1],
            device_id_type=LOGICAL,
        )

    def mask_start(stage):
        for d in (1, 2, 3):
            mask_copy(stage, d).start()

    def mask_wait(stage):
        for d in (1, 2, 3):
            mask_copy(stage, d).wait()

    mine = pl.ds(pl.multiple_of(shot * TS, TS), TS)

    def scatter(plane, dz, dx):
        ts = zs[dz] + xs[dx]
        pltpu.make_async_remote_copy(
            src_ref=spec.at[plane * NS + ts],
            dst_ref=grid.at[core, y, mine],
            send_sem=send1,
            recv_sem=recv1.at[y],
            device_id=ts * 8 + (plane * 2 + core),
            device_id_type=LOGICAL,
        ).start()

    pl.semaphore_wait(barrier, NS + 3)
    for d in (1, 2, 3):
        pl.semaphore_signal(ready.at[y], inc=1, device_id=shot * 8 + ys[d] * 2 + core, device_id_type=LOGICAL)
    mask_start(0)
    for dz, dx in PLANE:
        if dz or dx:
            scatter(y, dz, dx)
    pltpu.make_async_copy(spec.at[me], grid.at[core, y, mine], recv1.at[y]).start()
    for d in (2, 1, 3):
        pl.semaphore_wait(ready.at[ys[d]], 1)
        for dz, dx in PLANE:
            scatter(ys[d], dz, dx)
    mask_wait(0)
    mask_start(1)
    mask_wait(1)
    mask_start(2)

    block = lax.broadcasted_iota(jnp.int32, (128, 1024), 0)
    column = lax.broadcasted_iota(jnp.int32, (128, 1024), 1)
    tile = column % 512 // 128 * 2 + (column // 512 + core) % 2
    expand = jnp.where(block == 2 * tile + column % TR // TS, 1.0, 0.0).astype(jnp.bfloat16)
    def slab_copy(ty):
        return pltpu.make_async_remote_copy(
            src_ref=grid.at[core, ty],
            dst_ref=grid.at[core, ty],
            send_sem=xsend.at[ty],
            recv_sem=xrecv.at[ty],
            device_id=sibling,
            device_id_type=LOGICAL,
        )

    for d in (0, 2, 3, 1):
        slab = grid.at[core, ys[d]]
        pltpu.make_async_copy(slab, slab, recv1.at[ys[d]]).wait()
        slab_copy(ys[d]).start()

    mask_wait(2)
    mrow[...] = jnp.dot(
        mtab[...].reshape(CHIPS, 128).astype(jnp.bfloat16), expand, preferred_element_type=jnp.float32
    )

    def spread(t, carry):
        mask[t // NS, t % NS] = jnp.broadcast_to(mrow[pl.ds(t, 1), :], (16, 1024)).astype(jnp.bfloat16)
        return carry

    lax.fori_loop(0, CHIPS, spread, 0, unroll=4)

    left64 = lax.broadcasted_iota(jnp.int32, (TR, 128), 1) < TR

    def half(d, h):
        par = core if h == 0 else 1 - core
        for k in range(NY):
            cols = slice(k * 128, k * 128 + 128)
            left = grid[par, k].reshape(NS, 2, 16, 128)
            weights = mask[ys[d], :, :, h * 512 + k * 128 : h * 512 + k * 128 + 128]
            masked[:, cols] = (left * weights[:, None]).reshape(NS * TS, 128)
            first = pl.multiple_of((2 * k + par) * TR, TR)
            part = grid[core, ys[d], pl.ds(first, TR), :]
            turned = pltpu.roll(part.astype(jnp.float32), TR, 1)
            rhat[k * 128 : k * 128 + TR, :] = part
            rhat[k * 128 + TR : (k + 1) * 128, :] = jnp.where(left64, -turned, turned).astype(jnp.bfloat16)
        return jnp.dot(masked[...], rhat[...], preferred_element_type=jnp.float32)

    for d in range(NY):
        acc[d] = half(d, 0)
    for k in range(NY):
        other = grid.at[1 - core, k]
        pltpu.make_async_copy(other, other, xrecv.at[k]).wait()
    for d in BACK:
        ty = ys[d]
        prod[ty] = (acc[d] + half(d, 1)).astype(jnp.bfloat16)
        for dz, dx in [(a, b) for a in range(4) for b in (2, 1, 3, 0)]:
            ts = dz * 4 + xs[dx]
            give = pltpu.make_async_remote_copy(
                src_ref=prod.at[ty, pl.ds(pl.multiple_of(ts * TS, TS), TS)],
                dst_ref=back.at[y, shot],
                send_sem=send2,
                recv_sem=recv2,
                device_id=ts * 8 + (ty * 2 + core),
                device_id_type=LOGICAL,
            )
            if d:
                give.start()
            else:
                pl.when(ts != shot)(give.start)

    pltpu.make_async_copy(prod.at[y, mine], back.at[y, shot], recv2).start()
    pltpu.make_async_copy(back, back, recv2).wait()
    for k in range(NY):
        slab_copy(k).wait_send()
    sent = spec.at[pl.ds(0, CHIPS - 1)]
    pltpu.make_async_copy(sent, sent, send1).wait()
    pltpu.make_async_copy(sent, sent, send2).wait()


def widen(back, out, tiles, wide, in_sem, out_sem):
    loads = [pltpu.make_async_copy(back.at[k], tiles.at[k], in_sem.at[k]) for k in range(NY)]
    for load in loads:
        load.start()
    stores = []
    for k in range(NY):
        part = pl.ds(k * NS, NS)
        loads[k].wait()
        for n in range(NS):
            tile = tiles[k, n].astype(jnp.float32) * SCALE
            wide[k * NS + n, 0] = tile[:, :TR]
            wide[k * NS + n, 1] = pltpu.roll(tile, TR, 1)[:, :TR]
        stores.append(pltpu.make_async_copy(wide.at[part], out.at[part], out_sem.at[k]))
        stores[k].start()
    for store in stores:
        store.wait()


def local(traces, aperture_lists, aperture_counts):
    bf16, f32 = jnp.bfloat16, jnp.float32
    dma = pltpu.SemaphoreType.DMA
    back = pl.pallas_call(
        kernel,
        out_shape=jax.ShapeDtypeStruct((NY, NS, TS, 128), bf16),
        in_specs=[pl.BlockSpec(memory_space=pl.ANY)] * 3,
        out_specs=pl.BlockSpec(memory_space=pl.ANY),
        scratch_shapes=[
            pltpu.VMEM((TS, TR, NT), bf16),
            pltpu.VMEM((128, NT), bf16),
            pltpu.SMEM((1, 1, APB), jnp.int32),
            pltpu.VMEM((FREQS * PITCH, 128), f32),
            pltpu.VMEM((FREQS, TS, 128), bf16),
            pltpu.VMEM((2, NY, NS * TS, 128), bf16),
            pltpu.VMEM((CHIPS, 1, 128), f32),
            pltpu.VMEM((CHIPS, 1024), f32),
            pltpu.VMEM((NY, NS, 16, 1024), bf16),
            pltpu.VMEM((NS * TS, 512), bf16),
            pltpu.VMEM((512, 128), bf16),
            pltpu.VMEM((NY, NS * TS, 128), f32),
            pltpu.VMEM((NY, NS * TS, 128), bf16),
            dma((CHUNKS,)),
            dma,
            dma,
            dma,
            dma((NY,)),
            dma((NY,)),
            dma((NY,)),
            dma,
            dma,
            dma((9,)),
            dma((9,)),
            pltpu.SemaphoreType.REGULAR((4,)),
        ],
        compiler_params=pltpu.CompilerParams(
            collective_id=0, has_side_effects=True, vmem_limit_bytes=int(VMEM_MIB * 2**20)
        ),
        cost_estimate=pl.CostEstimate(flops=2**30, bytes_accessed=8 * 2**20, transcendentals=0),
        name="multiples",
    )(traces, jnp.asarray(dft_table()), aperture_lists)
    return pl.pallas_call(
        widen,
        out_shape=jax.ShapeDtypeStruct((FREQS, 2, TS, TR), f32),
        in_specs=[pl.BlockSpec(memory_space=pl.ANY)],
        out_specs=pl.BlockSpec(memory_space=pl.ANY),
        scratch_shapes=[
            pltpu.VMEM((NY, NS, TS, 128), bf16),
            pltpu.VMEM((FREQS, 2, TS, TR), f32),
            dma((NY,)),
            dma((NY,)),
        ],
        compiler_params=pltpu.CompilerParams(vmem_limit_bytes=int(VMEM_MIB * 2**20)),
        cost_estimate=pl.CostEstimate(flops=2**20, bytes_accessed=3 * 2**20, transcendentals=0),
        name="widen",
    )(back)


def solution(mesh):
    placed = (P("shot", "rcv", None), P("shot", "rcv", None), P("shot", "rcv"))
    return jax.shard_map(
        local, mesh=mesh, in_specs=placed, out_specs=P(None, None, "shot", "rcv"), check_vma=False
    )
```

```python
import math

import jax
import jax.numpy as jnp
import ml_dtypes
import numpy as np
from jax import lax
from jax.experimental import pallas as pl
from jax.experimental.pallas import tpu as pltpu
from jax.sharding import PartitionSpec as P

MESH = pl.DeviceIdType.MESH

NT = 1024
BAND = 32
APB = 8
FIRST = 32
SECOND = 128
FREQS = 64
TS = 32
TR = 64
NS = 16
NY = 4
CHIPS = 64
SCALE = 1.0 / math.sqrt(APB * TS)
CHUNKS = 2
PITCH = 40
VMEM_MIB = 60
BACK = (2, 1, 3, 0)
PLANE = [((a + b) % 4, b) for a in (2, 1, 3, 0) for b in (2, 1, 3, 0)]


def dft_table():
    sample = np.arange(NT)
    bins = np.concatenate([FIRST + np.arange(BAND), SECOND + np.arange(BAND)])
    phase = (bins[:, None] * sample[None, :] % NT).astype(np.float32) * np.float32(2.0 * math.pi / NT)
    phase = phase.astype(np.float64)
    factor = 1.0 / math.sqrt(NT)
    return (np.concatenate([np.cos(phase), -np.sin(phase)], axis=0) * factor).astype(np.float32).astype(
        ml_dtypes.bfloat16
    )


def kernel(
    traces,
    table_hbm,
    lists_hbm,
    back,
    tr,
    table,
    lists,
    specf,
    spec,
    grid,
    mtab,
    mrow,
    mask,
    masked,
    rhat,
    acc,
    prod,
    load_sem,
    table_sem,
    small_sem,
    send1,
    recv1,
    xsend,
    xrecv,
    send2,
    recv2,
    msend,
    mrecv,
    ready,
):
    shot = lax.axis_index("shot")
    rcv = lax.axis_index("rcv")
    y = rcv // 2
    core = rcv % 2
    z, x = shot // 4, shot % 4
    me = y * NS + shot
    sibling = (shot, y * 2 + 1 - core)
    zs = [(z + d) % 4 * 4 for d in range(4)]
    xs = [(x + d) % 4 for d in range(4)]
    ys = [(y + d) % 4 for d in range(4)]

    per = TS // CHUNKS
    loads = [
        pltpu.make_async_copy(traces.at[pl.ds(n * per, per)], tr.at[pl.ds(n * per, per)], load_sem.at[n])
        for n in range(CHUNKS)
    ]
    table_load = pltpu.make_async_copy(table_hbm, table, table_sem)
    lists_load = pltpu.make_async_copy(lists_hbm, lists, small_sem)
    table_load.start()
    for load in loads:
        load.start()
    lists_load.start()

    barrier = pltpu.get_barrier_semaphore()
    pl.semaphore_signal(barrier, inc=1, device_id=sibling, device_id_type=MESH)
    for d in (1, 2, 3):
        pl.semaphore_signal(
            barrier, inc=1, device_id=(shot, ys[d] * 2 + core), device_id_type=MESH
        )
    for dz, dx in PLANE:
        if dz or dx:
            pl.semaphore_signal(
                barrier, inc=1, device_id=(zs[dz] + xs[dx], rcv), device_id_type=MESH
            )

    lists_load.wait()
    lane = lax.broadcasted_iota(jnp.int32, (1, 128), 1)
    member = jnp.where(lane == lists[0, 0, 0], 1.0, 0.0)
    for k in range(1, APB):
        entry = lists[0, 0, k]
        block = jnp.where(entry == 0, -1, entry)
        member = jnp.where(lane == block, 1.0, member)
    mtab[me] = member

    low = lax.broadcasted_iota(jnp.int32, (FREQS, 128), 1) < TR
    table_load.wait()
    for n in range(CHUNKS):
        loads[n].wait()
        rows = tr[n * per : (n + 1) * per].reshape(per * TR, NT)
        flat = lax.dot_general(
            table[...], rows, (((1,), (1,)), ((), ())), preferred_element_type=jnp.float32
        )
        for p in range(per // 2):
            first = n * per + 2 * p
            re = flat[:FREQS, p * 128 : p * 128 + 128]
            im = flat[FREQS:, p * 128 : p * 128 + 128]
            specf[pl.ds(first, FREQS, stride=PITCH), :] = jnp.where(low, re, pltpu.roll(im, TR, 1))
            specf[pl.ds(first + 1, FREQS, stride=PITCH), :] = jnp.where(low, pltpu.roll(re, TR, 1), im)
    spec[...] = specf[...].reshape(FREQS, PITCH, 128)[:, :TS].astype(jnp.bfloat16)

    def mask_copy(stage, d):
        if stage == 0:
            rows, to = pl.ds(me, 1), (zs[0] + xs[d], rcv)
        elif stage == 1:
            rows, to = pl.ds(y * NS + z * 4, 4), (zs[d] + x, rcv)
        else:
            rows, to = pl.ds(y * NS, NS), (shot, ys[d] * 2 + core)
        return pltpu.make_async_remote_copy(
            src_ref=mtab.at[rows],
            dst_ref=mtab.at[rows],
            send_sem=msend.at[stage * 3 + d - 1],
            recv_sem=mrecv.at[stage * 3 + d - 1],
            device_id=to,
            device_id_type=MESH,
        )

    def mask_start(stage):
        for d in (1, 2, 3):
            mask_copy(stage, d).start()

    def mask_wait(stage):
        for d in (1, 2, 3):
            mask_copy(stage, d).wait()

    mine = pl.ds(pl.multiple_of(shot * TS, TS), TS)

    def scatter(plane, dz, dx):
        ts = zs[dz] + xs[dx]
        pltpu.make_async_remote_copy(
            src_ref=spec.at[plane * NS + ts],
            dst_ref=grid.at[core, y, mine],
            send_sem=send1,
            recv_sem=recv1.at[y],
            device_id=(ts, plane * 2 + core),
            device_id_type=MESH,
        ).start()

    pl.semaphore_wait(barrier, NS + 3)
    for d in (1, 2, 3):
        pl.semaphore_signal(ready.at[y], inc=1, device_id=(shot, ys[d] * 2 + core), device_id_type=MESH)
    mask_start(0)
    for dz, dx in PLANE:
        if dz or dx:
            scatter(y, dz, dx)
    pltpu.make_async_copy(spec.at[me], grid.at[core, y, mine], recv1.at[y]).start()
    for d in (2, 1, 3):
        pl.semaphore_wait(ready.at[ys[d]], 1)
        for dz, dx in PLANE:
            scatter(ys[d], dz, dx)
    mask_wait(0)
    mask_start(1)
    mask_wait(1)
    mask_start(2)

    block = lax.broadcasted_iota(jnp.int32, (128, 1024), 0)
    column = lax.broadcasted_iota(jnp.int32, (128, 1024), 1)
    tile = column % 512 // 128 * 2 + (column // 512 + core) % 2
    expand = jnp.where(block == 2 * tile + column % TR // TS, 1.0, 0.0).astype(jnp.bfloat16)
    def slab_copy(ty):
        return pltpu.make_async_remote_copy(
            src_ref=grid.at[core, ty],
            dst_ref=grid.at[core, ty],
            send_sem=xsend.at[ty],
            recv_sem=xrecv.at[ty],
            device_id=sibling,
            device_id_type=MESH,
        )

    for d in (0, 2, 3, 1):
        slab = grid.at[core, ys[d]]
        pltpu.make_async_copy(slab, slab, recv1.at[ys[d]]).wait()
        slab_copy(ys[d]).start()

    mask_wait(2)
    mrow[...] = jnp.dot(
        mtab[...].reshape(CHIPS, 128).astype(jnp.bfloat16), expand, preferred_element_type=jnp.float32
    )

    def spread(t, carry):
        mask[t // NS, t % NS] = jnp.broadcast_to(mrow[pl.ds(t, 1), :], (16, 1024)).astype(jnp.bfloat16)
        return carry

    lax.fori_loop(0, CHIPS, spread, 0, unroll=4)

    left64 = lax.broadcasted_iota(jnp.int32, (TR, 128), 1) < TR

    def half(d, h):
        par = core if h == 0 else 1 - core
        for k in range(NY):
            cols = slice(k * 128, k * 128 + 128)
            left = grid[par, k].reshape(NS, 2, 16, 128)
            weights = mask[ys[d], :, :, h * 512 + k * 128 : h * 512 + k * 128 + 128]
            masked[:, cols] = (left * weights[:, None]).reshape(NS * TS, 128)
            first = pl.multiple_of((2 * k + par) * TR, TR)
            part = grid[core, ys[d], pl.ds(first, TR), :]
            turned = pltpu.roll(part.astype(jnp.float32), TR, 1)
            rhat[k * 128 : k * 128 + TR, :] = part
            rhat[k * 128 + TR : (k + 1) * 128, :] = jnp.where(left64, -turned, turned).astype(jnp.bfloat16)
        return jnp.dot(masked[...], rhat[...], preferred_element_type=jnp.float32)

    for d in range(NY):
        acc[d] = half(d, 0)
    for k in range(NY):
        other = grid.at[1 - core, k]
        pltpu.make_async_copy(other, other, xrecv.at[k]).wait()
    for d in BACK:
        ty = ys[d]
        prod[ty] = (acc[d] + half(d, 1)).astype(jnp.bfloat16)
        for dz, dx in [(a, b) for a in range(4) for b in (2, 1, 3, 0)]:
            ts = dz * 4 + xs[dx]

            @pl.when(jnp.logical_or(ts != shot, ty != y))
            def _():
                pltpu.make_async_remote_copy(
                    src_ref=prod.at[ty, pl.ds(pl.multiple_of(ts * TS, TS), TS)],
                    dst_ref=back.at[y, shot],
                    send_sem=send2,
                    recv_sem=recv2,
                    device_id=(ts, ty * 2 + core),
                    device_id_type=MESH,
                ).start()

    pltpu.make_async_copy(prod.at[y, mine], back.at[y, shot], recv2).start()
    pltpu.make_async_copy(back, back, recv2).wait()
    for k in range(NY):
        slab_copy(k).wait_send()
    sent = spec.at[pl.ds(0, CHIPS - 1)]
    pltpu.make_async_copy(sent, sent, send1).wait()
    pltpu.make_async_copy(sent, sent, send2).wait()


def widen(back, out, tiles, wide, in_sem, out_sem):
    loads = [pltpu.make_async_copy(back.at[k], tiles.at[k], in_sem.at[k]) for k in range(NY)]
    for load in loads:
        load.start()
    stores = []
    for k in range(NY):
        part = pl.ds(k * NS, NS)
        loads[k].wait()
        for n in range(NS):
            tile = tiles[k, n].astype(jnp.float32) * SCALE
            wide[k * NS + n, 0] = tile[:, :TR]
            wide[k * NS + n, 1] = pltpu.roll(tile, TR, 1)[:, :TR]
        stores.append(pltpu.make_async_copy(wide.at[part], out.at[part], out_sem.at[k]))
        stores[k].start()
    for store in stores:
        store.wait()


def local(traces, aperture_lists, aperture_counts):
    bf16, f32 = jnp.bfloat16, jnp.float32
    dma = pltpu.SemaphoreType.DMA
    back = pl.pallas_call(
        kernel,
        out_shape=jax.ShapeDtypeStruct((NY, NS, TS, 128), bf16),
        in_specs=[pl.BlockSpec(memory_space=pl.ANY)] * 3,
        out_specs=pl.BlockSpec(memory_space=pl.ANY),
        scratch_shapes=[
            pltpu.VMEM((TS, TR, NT), bf16),
            pltpu.VMEM((128, NT), bf16),
            pltpu.SMEM((1, 1, APB), jnp.int32),
            pltpu.VMEM((FREQS * PITCH, 128), f32),
            pltpu.VMEM((FREQS, TS, 128), bf16),
            pltpu.VMEM((2, NY, NS * TS, 128), bf16),
            pltpu.VMEM((CHIPS, 1, 128), f32),
            pltpu.VMEM((CHIPS, 1024), f32),
            pltpu.VMEM((NY, NS, 16, 1024), bf16),
            pltpu.VMEM((NS * TS, 512), bf16),
            pltpu.VMEM((512, 128), bf16),
            pltpu.VMEM((NY, NS * TS, 128), f32),
            pltpu.VMEM((NY, NS * TS, 128), bf16),
            dma((CHUNKS,)),
            dma,
            dma,
            dma,
            dma((NY,)),
            dma((NY,)),
            dma((NY,)),
            dma,
            dma,
            dma((9,)),
            dma((9,)),
            pltpu.SemaphoreType.REGULAR((4,)),
        ],
        compiler_params=pltpu.CompilerParams(
            collective_id=0, has_side_effects=True, vmem_limit_bytes=int(VMEM_MIB * 2**20)
        ),
        cost_estimate=pl.CostEstimate(flops=2**30, bytes_accessed=8 * 2**20, transcendentals=0),
        name="multiples",
    )(traces, jnp.asarray(dft_table()), aperture_lists)
    return pl.pallas_call(
        widen,
        out_shape=jax.ShapeDtypeStruct((FREQS, 2, TS, TR), f32),
        in_specs=[pl.BlockSpec(memory_space=pl.ANY)],
        out_specs=pl.BlockSpec(memory_space=pl.ANY),
        scratch_shapes=[
            pltpu.VMEM((NY, NS, TS, 128), bf16),
            pltpu.VMEM((FREQS, 2, TS, TR), f32),
            dma((NY,)),
            dma((NY,)),
        ],
        compiler_params=pltpu.CompilerParams(vmem_limit_bytes=int(VMEM_MIB * 2**20)),
        cost_estimate=pl.CostEstimate(flops=2**20, bytes_accessed=3 * 2**20, transcendentals=0),
        name="widen",
    )(back)


def solution(mesh):
    placed = (P("shot", "rcv", None), P("shot", "rcv", None), P("shot", "rcv"))
    return jax.shard_map(
        local, mesh=mesh, in_specs=placed, out_specs=P(None, None, "shot", "rcv"), check_vma=False
    )
```
